32 devices in a mesh: pt: 4 (over z), comp: 8 (over y, x, core).
Axes of the slice: x: 2, y: 2, z: 4, core: 2. Of those that a mesh axis runs over, the one named last changes fastest.
Arguments:
- spectrum: float32 [512, 131072], P(None, ('pt', 'comp')), may hold values from 0.1 to 2
- wind: float32 [131072], P(('pt', 'comp')), may hold values from 0.5 to 4
- growth: float32 [512], replicated, may hold values from 0.05 to 0.5
- whitecap: float32 [512], replicated, may hold values from 0.1 to 1
- courant: float32 [16], replicated, may hold values from 0.2 to 0.7
- substeps: int32 [512], replicated, may hold values from 1 to 8, as said below
- limiter: int32 [131072], P(('pt', 'comp')), may hold values 0 or 1
- deck: int32 [131072], replicated, may hold values from 0 to 131071, as said below
- wet: int32 [256, 512], replicated, may hold values 0 or 1
Outputs:
- spectrum_out: float32 [512, 131072], P(None, ('pt', 'comp'))
- height: float32 [131072], P(('pt', 'comp'))
The draws below stay inside these ranges and needn't reach their ends.
Inputs may be any that keep to these rules, and one draw needn't show every extreme that they name: Every component has 1 to 8 substeps, and some component has exactly 8. Each grid cell appears at exactly one deck slot. The deck is dealt in aligned runs of 128 slots: slots k * 128 .. k * 128 + 127 hold 128 consecutive cells, in order, starting at a multiple of 128.
All inputs are finite; a program needn't handle non-finite values. No bound on the sum of `limiter` on one device may be relied on, other than what follows from the above.
Results may differ from the reference program's by a relative error of at most 0.0003.
Values sent between devices are 32-bit elements; how exact they have to be, the bound alone decides.
No kernel may reach another device: no remote copies, remote signals or barrier semaphores. Data moves between devices by JAX's collectives and lax.ppermute only.
A program may use at most 128 MiB of HBM per device.

```python
import math
import jax
import jax.numpy as jnp
from jax import lax

DIRS = 32
FREQ = 16
GX = 256
GY = 512
MAXSUB = 8
RUN = 128
COMP = 512
NPTS = 131072


def draw_substeps(key, part):
    counts = jax.random.randint(key, (COMP,), 1, MAXSUB + 1)
    chosen = jax.random.randint(jax.random.fold_in(key, 7), (), 0, COMP)
    return counts.at[chosen].set(MAXSUB).astype(jnp.int32)


def draw_deck(key, part):
    run_count = NPTS // RUN
    shuffled = jax.random.permutation(jax.random.fold_in(key, 11), run_count).astype(jnp.int32)
    offsets = jnp.arange(RUN, dtype=jnp.int32)
    return (shuffled[:, None] * RUN + offsets[None, :]).reshape(NPTS).astype(jnp.int32)


def place_ends(drawn, key, low, largest):
    shape = drawn.shape
    spot = [jax.random.randint(jax.random.fold_in(key, axis), (), 0, shape[axis]) for axis in range(len(shape))]
    drawn = drawn.at[tuple(spot)].set(low)
    longest = shape.index(max(shape))
    spot[longest] = (spot[longest] + 1) % shape[longest]
    return drawn.at[tuple(spot)].set(largest)


def level_of(stream_key, dims, cuts, smallest, largest):
    gain, own = 1.0, jax.random.fold_in(stream_key, 6)
    for dim, blocks in cuts:
        draws = jnp.exp(jax.random.uniform(jax.random.fold_in(own, dim), (blocks,), jnp.float32, smallest / len(cuts), largest / len(cuts)))
        gain = gain * jnp.repeat(draws, dims[dim] // blocks).reshape([-1 if axis == dim else 1 for axis in range(len(dims))])
    return gain


def setup_inputs(seed: int = 0) -> dict:
    seeds = jax.random.split(jax.random.key(seed), 10)
    return {
        "spectrum": jnp.clip(jnp.exp(math.log(2.0) - 2.9957323 * jax.random.uniform(seeds[0], (COMP, NPTS), jnp.float32) ** level_of(seeds[0], (COMP, NPTS), ((1, 32),), -0.2, 0.2)), 0.1, 2.0),
        "wind": jnp.clip(jnp.exp(math.log(4.0) - 2.0794415 * jax.random.uniform(seeds[1], (NPTS,), jnp.float32) ** level_of(seeds[1], (NPTS,), ((0, 32),), -0.2, 0.2)), 0.5, 4.0),
        "growth": jnp.clip(jnp.exp(jax.random.uniform(seeds[2], (COMP,), jnp.float32, math.log(0.05), math.log(0.5))), 0.05, 0.5),
        "whitecap": jnp.clip(jnp.exp(jax.random.uniform(seeds[3], (COMP,), jnp.float32, math.log(0.1), math.log(1.0))), 0.1, 1.0),
        "courant": jnp.clip(jnp.exp(jax.random.uniform(seeds[4], (FREQ,), jnp.float32, math.log(0.2), math.log(0.7))), 0.2, 0.7),
        "substeps": draw_substeps(jax.random.fold_in(seeds[9], 71), 0),
        "limiter": place_ends((jax.random.randint(seeds[6], (NPTS,), 0, 3) < 1).astype(jnp.int32), jax.random.fold_in(seeds[6], 1), 0, 1),
        "deck": draw_deck(jax.random.fold_in(seeds[9], 71), 0),
        "wet": place_ends((jax.random.randint(seeds[8], (GX, GY), 0, 4) < 3).astype(jnp.int32), jax.random.fold_in(seeds[8], 1), 0, 1),
    }


rate_limit = 0.5
time_step = 0.5

def sources(spectrum, wind, growth, whitecap, limiter):
    mean_energy = lax.optimization_barrier(jnp.mean(spectrum, axis=0))
    rate = wind[None, :] * growth[:, None] - whitecap[:, None] * (mean_energy / (1.0 + mean_energy))[None, :]
    rate = jnp.where(limiter[None, :] == 1, rate_limit * jnp.tanh(rate / rate_limit), rate)
    return spectrum * jnp.exp(time_step * rate)

def substep(field_grid, cross, along, wetness):
    sea = field_grid * wetness[None, :, :]
    east = jnp.roll(sea, 1, axis=2)
    west = jnp.roll(sea, -1, axis=2)
    up_column = jnp.where(along[:, None, None] > 0, east, west)
    zero_row = jnp.zeros_like(sea[:, :1, :])
    south = jnp.concatenate([zero_row, sea[:, :-1, :]], axis=1)
    north = jnp.concatenate([sea[:, 1:, :], zero_row], axis=1)
    up_row = jnp.where(cross[:, None, None] > 0, south, north)
    moved = field_grid - jnp.abs(cross)[:, None, None] * (field_grid - up_row) - jnp.abs(along)[:, None, None] * (field_grid - up_column)
    return jnp.where(wetness[None, :, :] > 0, moved, field_grid)

def reference(spectrum, wind, growth, whitecap, courant, substeps, limiter, deck, wet):
    forced = sources(spectrum, wind, growth, whitecap, limiter)
    inverse = jnp.zeros((NPTS,), jnp.int32).at[deck].set(jnp.arange(NPTS, dtype=jnp.int32))
    wetness = wet.astype(jnp.float32)
    comps = jnp.arange(COMP, dtype=jnp.int32)
    angle = 2.0 * math.pi / DIRS * ((comps % DIRS).astype(jnp.float32) + 0.5)
    speed = courant[comps // DIRS]
    cross = speed * jnp.sin(angle)
    along = speed * jnp.cos(angle)

    def block(items):
        fields, cr, al, counts = items
        field_grid = fields[:, inverse].reshape(-1, GX, GY)
        for step in range(MAXSUB):
            field_grid = jnp.where(step < counts[:, None, None], substep(field_grid, cr, al, wetness), field_grid)
        return field_grid.reshape(-1, NPTS)[:, deck]
    blocks = COMP // 16
    result = lax.map(block, (forced.reshape(blocks, 16, NPTS), cross.reshape(blocks, 16), along.reshape(blocks, 16), substeps.reshape(blocks, 16)))
    spectrum_out = result.reshape(COMP, NPTS)
    height = 4.0 * jnp.sqrt(lax.optimization_barrier(jnp.mean(spectrum_out, axis=0)) + 1e-06)
    return (spectrum_out, height)
```

```python
import math

import jax
import jax.numpy as jnp
from jax import lax
from jax.experimental import pallas as pl
from jax.experimental.pallas import tpu as pltpu
from jax.sharding import PartitionSpec as P

DIRS = 32
MAXSUB = 8
RUN = 128
SUB = 8

rate_limit = 0.5
time_step = 0.5

MIB = 1024 * 1024


def plain_sources(spectrum, wind, growth, whitecap, limiter):
    mean_energy = jnp.mean(spectrum, axis=0)
    rate = (
        wind[None, :] * growth[:, None]
        - whitecap[:, None] * (mean_energy / (1.0 + mean_energy))[None, :]
    )
    rate = jnp.where(limiter[None, :] == 1, rate_limit * jnp.tanh(rate / rate_limit), rate)
    return spectrum * jnp.exp(time_step * rate)


def plain_substep(field_grid, cross, along, wetness):
    sea = field_grid * wetness[None, :, :]
    east = jnp.roll(sea, 1, axis=2)
    west = jnp.roll(sea, -1, axis=2)
    up_column = jnp.where(along[:, None, None] > 0, east, west)
    zero_row = jnp.zeros_like(sea[:, :1, :])
    south = jnp.concatenate([zero_row, sea[:, :-1, :]], axis=1)
    north = jnp.concatenate([sea[:, 1:, :], zero_row], axis=1)
    up_row = jnp.where(cross[:, None, None] > 0, south, north)
    moved = (
        field_grid
        - jnp.abs(cross)[:, None, None] * (field_grid - up_row)
        - jnp.abs(along)[:, None, None] * (field_grid - up_column)
    )
    return jnp.where(wetness[None, :, :] > 0, moved, field_grid)


def plain(spectrum, wind, growth, whitecap, courant, substeps, limiter, deck, wet):
    forced = plain_sources(spectrum, wind, growth, whitecap, limiter)
    comp_count = lax.axis_size("comp")
    group_size = lax.axis_size("pt") * comp_count
    total_comps, point_count = forced.shape
    per_device = total_comps // group_size
    all_points = deck.shape[0]
    rows_grid, cols_grid = wet.shape
    run_count = all_points // RUN
    received = lax.all_to_all(
        forced.reshape(per_device, group_size, point_count),
        ("pt", "comp"),
        split_axis=1,
        concat_axis=1,
        tiled=True,
    )
    fields = received.reshape(per_device, run_count, RUN)
    own_rank = lax.axis_index("pt") * comp_count + lax.axis_index("comp")
    comps = jnp.arange(per_device, dtype=jnp.int32) * group_size + own_rank
    cross, along = courants(comps, courant)
    counts = substeps[comps]
    wetness = wet.astype(jnp.float32)
    slot_runs = deck.reshape(run_count, RUN)[:, 0] // RUN
    cell_runs = jnp.zeros((run_count,), jnp.int32).at[slot_runs].set(
        jnp.arange(run_count, dtype=jnp.int32)
    )
    field_grid = jnp.take(fields, cell_runs, axis=1).reshape(per_device, rows_grid, cols_grid)
    for step in range(MAXSUB):
        field_grid = jnp.where(
            step < counts[:, None, None],
            plain_substep(field_grid, cross, along, wetness),
            field_grid,
        )
    slots = jnp.take(field_grid.reshape(per_device, run_count, RUN), slot_runs, axis=1)
    back = lax.all_to_all(
        slots.reshape(per_device, group_size, point_count),
        ("pt", "comp"),
        split_axis=1,
        concat_axis=1,
        tiled=True,
    )
    arrived = back.reshape(total_comps, point_count)
    height = 4.0 * jnp.sqrt(jnp.mean(arrived, axis=0) + 1e-06)
    return (arrived, height)


def courants(comps, courant):
    angle = 2.0 * math.pi / DIRS * ((comps % DIRS).astype(jnp.float32) + 0.5)
    speed = courant[comps // DIRS]
    return speed * jnp.sin(angle), speed * jnp.cos(angle)


def lane_gather(x, idx):
    dims = lax.GatherDimensionNumbers(
        offset_dims=(),
        collapsed_slice_dims=(1,),
        start_index_map=(1,),
        operand_batching_dims=(0,),
        start_indices_batching_dims=(0,),
    )
    return lax.gather(
        x, idx[..., None], dims, slice_sizes=(1, 1), mode=lax.GatherScatterMode.PROMISE_IN_BOUNDS
    )


def lanes(rows=SUB):
    return lax.broadcasted_iota(jnp.int32, (rows, RUN), 1)


def rows_of(block, j):
    return jnp.broadcast_to(block[j : j + 1, :], (SUB, RUN))


def place(off, cap):
    first = jnp.minimum(off // RUN, cap - 1)
    return first, off - first * RUN


def columns(t):
    return slice(t * RUN, (t + 1) * RUN)


def write_stream(values, spots, lane, store, cap):
    merged = values[0]
    for t, (value, (first, start)) in enumerate(zip(values, spots)):
        if t > 0:
            before = jnp.where(first == spots[t - 1][0], merged, values[t - 1])
            merged = jnp.where(lane >= start, value, before)
        if t == len(values) - 1:
            store(jnp.minimum(first + 1, cap - 1), value)
        store(first, merged)


def force(value, wind, ratio, limited, growth, whitecap):
    rate = wind * growth - whitecap * ratio
    rate = jnp.where(limited, rate_limit * jnp.tanh(rate / rate_limit), rate)
    return value * jnp.exp(time_step * rate)


def spread(row):
    return jnp.transpose(jnp.broadcast_to(row, (RUN, RUN)))


def begin_kernel(
    small, runs, row_runs, rank, deck, wet, wind, limiter, growth, whitecap, spectrum,
    held, sent_small, sent_full, idxu, idxp, offs, own_idxu, own_idxp, own_off, ratio, need,
    values, packed, sea, total, grown, capped, off, in_sems, held_sems, sent_sems, off_sem,
):
    comps = values.shape[0]
    slots = deck.shape[0]
    groups = packed.shape[0] // runs
    parts = in_sems.shape[0]
    part = comps // parts

    def fetch(p):
        rows = pl.ds(p * part, part)
        return pltpu.make_async_copy(spectrum.at[rows], values.at[rows], in_sems.at[p])

    for p in range(parts):
        fetch(p).start()

    halves = wet.shape[0] // RUN
    for q in range(row_runs):
        for h in range(halves):
            k = q * halves + h
            sea[k * RUN : (k + 1) * RUN, :] = wet[h * RUN : (h + 1) * RUN, columns(q)].astype(
                jnp.float32
            ).astype(jnp.bfloat16)

    lane = lanes(RUN)
    row = lax.broadcasted_iota(jnp.int32, (RUN, RUN), 0)
    one = lambda mask: jnp.where(mask, 1.0, 0.0).astype(jnp.bfloat16)
    earlier = one(row < lane)
    ones = jnp.ones((RUN, RUN), jnp.bfloat16)
    runs_before = one((lane < row) & (lane // runs == row // runs))
    dot = lambda a, b: jnp.dot(a, b, preferred_element_type=jnp.float32)

    def tables(b, most):
        here = pl.ds(pl.multiple_of(b * RUN, RUN), RUN)
        slot = deck[here, :] // RUN
        picks = [
            one(slot == lane * row_runs + (h * RUN * row_runs + q))
            for q in range(row_runs)
            for h in range(halves)
        ]
        wet_here = dot(jnp.concatenate(picks, axis=1), sea[...])
        wet_low = wet_here.astype(jnp.bfloat16)
        prefix = dot(wet_low, earlier)
        count = dot(wet_low, ones)
        off_f = dot(runs_before, count.astype(jnp.bfloat16))
        off_i = off_f.astype(jnp.int32)
        through = (prefix + wet_here).astype(jnp.int32)
        spot = jnp.bitwise_and(off_i + prefix.astype(jnp.int32), RUN - 1)
        idxu[here, :] = jnp.where(wet_here > 0.5, spot, spot + RUN)
        offs[here, :] = off_i
        nth = jnp.bitwise_and(lane - off_i, RUN - 1)
        at = jnp.zeros((RUN, RUN), jnp.int32)
        bit = RUN // 2
        while bit:
            probe = lane_gather(through, at + (bit - 1))
            at = jnp.where(probe <= nth, at + bit, at)
            bit //= 2
        idxp[here, :] = at
        return jnp.maximum(most, jnp.max(off_f + count))

    most = lax.fori_loop(0, slots // RUN, tables, jnp.float32(0)).astype(jnp.int32)
    need[0] = most
    mine = pl.ds(pl.multiple_of(rank[0] * runs, SUB), runs)
    own_idxu[...] = idxu[mine, :]
    own_idxp[...] = idxp[mine, :]
    own_off[...] = offs[mine, :]
    off_copy = pltpu.make_async_copy(own_off, off, off_sem)
    off_copy.start()

    for r in range(grown.shape[0] // RUN):
        rows = slice(r * RUN, (r + 1) * RUN)
        grown[rows, :] = spread(growth[r : r + 1, :])
        capped[rows, :] = spread(whitecap[r : r + 1, :])

    for p in range(parts):
        fetch(p).wait()
        for t in range(runs):
            cols = columns(t)
            added = [values[p * part + g * SUB : p * part + (g + 1) * SUB, cols] for g in range(part // SUB)]
            while len(added) > 1:
                added = [sum(added[k : k + 2]) for k in range(0, len(added), 2)]
            total[:, cols] = added[0] if p == 0 else total[:, cols] + added[0]
    mean = jnp.sum(total[...], axis=0, keepdims=True) / comps
    ratio[...] = jnp.broadcast_to(mean / (1.0 + mean), ratio.shape)

    off_copy.wait()
    cap = jnp.where(most <= small * RUN, small, runs)
    reg_lane = lanes()

    def keep(g):
        rows = pl.ds(pl.multiple_of(g * SUB, SUB), SUB)
        return pltpu.make_async_copy(values.at[rows], held.at[rows], held_sems.at[g])

    def pass_on(g, size, target):
        regs = pl.ds(g * size, size)
        return pltpu.make_async_copy(packed.at[regs], target.at[regs], sent_sems.at[g])

    def group(g, carry):
        rows = pl.ds(pl.multiple_of(g * SUB, SUB), SUB)
        growth_g = grown[rows, :]
        whitecap_g = capped[rows, :]
        forced = []
        for t in range(runs):
            cols = columns(t)
            wind_t = jnp.broadcast_to(wind[:, cols], (SUB, RUN))
            limited = jnp.broadcast_to(limiter[:, cols], (SUB, RUN)) == 1
            forced.append(force(values[rows, cols], wind_t, ratio[:, cols], limited, growth_g, whitecap_g))
        for t in range(runs):
            values[rows, columns(t)] = forced[t]
        keep(g).start()
        sent = [lane_gather(forced[t], rows_of(own_idxp, t)) for t in range(runs)]
        spots = [place(off[t, 0], cap) for t in range(runs)]

        def store(at, value):
            packed[g * cap + at] = value

        write_stream(sent, spots, reg_lane, store, cap)

        @pl.when(most <= small * RUN)
        def _():
            pass_on(g, small, sent_small).start()

        @pl.when(most > small * RUN)
        def _():
            pass_on(g, runs, sent_full).start()

        return carry

    lax.fori_loop(0, groups, group, 0)

    def drain(g, carry):
        keep(g).wait()

        @pl.when(most <= small * RUN)
        def _():
            pass_on(g, small, sent_small).wait()

        @pl.when(most > small * RUN)
        def _():
            pass_on(g, runs, sent_full).wait()

        return carry

    lax.fori_loop(0, groups, drain, 0)


def begin(small, runs, row_runs, groups, rank, deck, wet, wind, limiter, growth, whitecap, spectrum):
    comps, points = spectrum.shape
    slots = deck.shape[0]
    block = groups * SUB
    parts = 8
    smem = pl.BlockSpec(memory_space=pltpu.SMEM)
    vmem = pl.BlockSpec(memory_space=pltpu.VMEM)
    far = pl.BlockSpec(memory_space=pl.ANY)
    cells = comps * points
    f32 = lambda *shape: jax.ShapeDtypeStruct(shape, jnp.float32)
    i32 = lambda *shape: jax.ShapeDtypeStruct(shape, jnp.int32)

    def body(*refs):
        begin_kernel(small, runs, row_runs, *refs)

    return pl.pallas_call(
        body,
        in_specs=[smem, vmem, vmem, vmem, vmem, vmem, vmem, far],
        out_specs=[far] * 3 + [vmem] * 7 + [smem],
        out_shape=[
            f32(block, points),
            f32(groups * small, SUB, RUN),
            f32(groups * runs, SUB, RUN),
            i32(slots, RUN),
            i32(slots, RUN),
            i32(slots, RUN),
            i32(runs, RUN),
            i32(runs, RUN),
            i32(runs, RUN),
            f32(SUB, points),
            i32(1),
        ],
        scratch_shapes=[
            pltpu.VMEM((comps, points), jnp.float32),
            pltpu.VMEM((groups * runs, SUB, RUN), jnp.float32),
            pltpu.VMEM((slots, RUN), jnp.bfloat16),
            pltpu.VMEM((SUB, points), jnp.float32),
            pltpu.VMEM((block, RUN), jnp.float32),
            pltpu.VMEM((block, RUN), jnp.float32),
            pltpu.SMEM((runs, RUN), jnp.int32),
            pltpu.SemaphoreType.DMA((parts,)),
            pltpu.SemaphoreType.DMA((groups,)),
            pltpu.SemaphoreType.DMA((groups,)),
            pltpu.SemaphoreType.DMA,
        ],
        cost_estimate=pl.CostEstimate(flops=10 * cells, bytes_accessed=10 * cells, transcendentals=cells),
        compiler_params=pltpu.CompilerParams(vmem_limit_bytes=32 * MIB),
        name="begin",
    )(rank, deck, wet, wind, limiter, growth, whitecap, spectrum)


def source_kernel(cap, runs, off, wind, limiter, ratio, growth, whitecap, idxp, spectrum, forced, packed):
    groups = spectrum.shape[0] // SUB
    lane = lanes()
    block = groups * SUB
    step = pl.program_id(0)
    grown = spread(growth[...].reshape(1, RUN))
    capped = spread(whitecap[...].reshape(1, RUN))
    spots = [place(off[t, 0], cap) for t in range(runs)]
    for g in range(groups):
        rows = slice(g * SUB, (g + 1) * SUB)
        values = []
        for t in range(runs):
            cols = columns(t)
            wind_t = jnp.broadcast_to(wind[:, cols], (SUB, RUN))
            limited = jnp.broadcast_to(limiter[:, cols], (SUB, RUN)) == 1
            values.append(
                force(spectrum[rows, cols], wind_t, ratio[:, cols], limited, grown[rows, :], capped[rows, :])
            )
        for t in range(runs):
            forced[rows, columns(t)] = values[t]
        sent = [lane_gather(values[t], rows_of(idxp, t)) for t in range(runs)]

        def store(at, value, g=g):
            packed[g, at] = value

        write_stream(sent, spots, lane, store, cap)


def sources(cap, chunk, groups, off, wind, limiter, ratio, growth, whitecap, idxp, spectrum):
    points = spectrum.shape[1]
    runs = points // RUN
    block = RUN
    block_groups = block // SUB
    steps = groups // block_groups
    base = chunk * steps
    whole = lambda i: (0, 0)
    cells = groups * SUB * points

    def body(*refs):
        source_kernel(cap, runs, *refs)

    return pl.pallas_call(
        body,
        grid=(steps,),
        in_specs=[
            pl.BlockSpec(memory_space=pltpu.SMEM),
            pl.BlockSpec((1, points), whole),
            pl.BlockSpec((1, points), whole),
            pl.BlockSpec((SUB, points), whole),
            pl.BlockSpec((1, 1, RUN), lambda i: (base + i, 0, 0)),
            pl.BlockSpec((1, 1, RUN), lambda i: (base + i, 0, 0)),
            pl.BlockSpec((runs, RUN), whole),
            pl.BlockSpec((block, points), lambda i: (base + i, 0)),
        ],
        out_specs=[
            pl.BlockSpec((block, points), lambda i: (i, 0)),
            pl.BlockSpec((block_groups, cap, SUB, RUN), lambda i: (i, 0, 0, 0)),
        ],
        out_shape=[
            jax.ShapeDtypeStruct((groups * SUB, points), jnp.float32),
            jax.ShapeDtypeStruct((groups, cap, SUB, RUN), jnp.float32),
        ],
        cost_estimate=pl.CostEstimate(flops=10 * cells, bytes_accessed=12 * cells, transcendentals=2 * cells),
        compiler_params=pltpu.CompilerParams(vmem_limit_bytes=24 * MIB),
        name="sources",
    )(off, wind, limiter, ratio, growth[:, None, :], whitecap[:, None, :], idxp, spectrum)


def propagate_kernel(
    cap, runs, row_runs, slot, off, info, recv, idxu, idxp, wet, cx, cy, counts, sent, field, other, wide
):
    total = slot.shape[0]
    lane = lanes()
    blank = jnp.zeros((SUB, RUN), jnp.float32)
    for ref in (field, other):
        for q in range(row_runs):
            ref[q] = blank
            ref[row_runs + total + q] = blank

    span = 4 * SUB

    def spread_wet(i, carry):
        t0 = pl.multiple_of(i * span, SUB)
        block = wet[pl.ds(t0, span), :].astype(jnp.float32)
        for j in range(span):
            wide[t0 + j] = rows_of(block, j)
        return carry

    lax.fori_loop(0, total // span, spread_wet, 0)

    def unpack(i, carry):
        t0 = pl.multiple_of(i * runs, SUB)
        base = i * cap
        indices = idxu[pl.ds(t0, runs), :]
        done = []
        for j in range(runs):
            first, start = place(off[t0 + j], cap)
            second = jnp.minimum(first + 1, cap - 1)
            window = jnp.where(lane >= start, recv[base + first], recv[base + second])
            index = rows_of(indices, j)
            cells = lane_gather(window, jnp.bitwise_and(index, RUN - 1))
            done.append(jnp.where(index < RUN, cells, 0.0))
        for j in range(runs):
            field[row_runs + slot[t0 + j]] = done[j]
        return carry

    lax.fori_loop(0, total // runs, unpack, 0)

    up_row = info[0]
    last = info[2]
    block = 32 * row_runs

    def run_steps(eastward):
        edge = lane == (0 if eastward else RUN - 1)
        shift = 1 if eastward else RUN - 1

        def step(n, src, dst):
            on = n < counts[...]
            b = jnp.where(on, cx[...], 0.0)
            c = jnp.where(on, cy[...], 0.0)
            a = 1.0 - b - c

            def rows(i, inner):
                t0 = i * block
                here = src[pl.ds(row_runs + t0, block)]
                up_x = src[pl.ds(row_runs + t0 + up_row, block)]
                sea = wide[pl.ds(t0, block)]
                rolled = [pltpu.roll(here[k], shift, 1) for k in range(block)]
                out = []
                for k in range(block):
                    q = k % row_runs
                    near = rolled[k - q + (q - 1 if eastward else q + 1) % row_runs]
                    up_y = jnp.where(edge, near, rolled[k])
                    out.append(sea[k] * (a * here[k] + b * up_x[k] + c * up_y))
                dst[pl.ds(row_runs + t0, block)] = jnp.stack(out)
                return inner

            lax.fori_loop(0, total // block, rows, 0)

        def pair(m, carry):
            step(2 * m, field, other)
            step(2 * m + 1, other, field)
            return carry

        lax.fori_loop(0, (last + 1) // 2, pair, 0)

    @pl.when(info[1] > 0)
    def _():
        run_steps(True)

    @pl.when(info[1] <= 0)
    def _():
        run_steps(False)

    def pack(i, carry):
        t0 = pl.multiple_of(i * runs, SUB)
        indices = idxp[pl.ds(t0, runs), :]
        picked = [
            lane_gather(field[row_runs + slot[t0 + j]], rows_of(indices, j)) for j in range(runs)
        ]
        spots = [place(off[t0 + j], cap) for j in range(runs)]

        def store(at, value):
            sent[i * cap + at] = value

        write_stream(picked, spots, lane, store, cap)
        return carry

    lax.fori_loop(0, total // runs, pack, 0)


def propagate(cap, runs, row_runs, slot, off, info, recv, idxu, idxp, wet, cx, cy, counts):
    total = slot.shape[0]
    smem = pl.BlockSpec(memory_space=pltpu.SMEM)
    vmem = pl.BlockSpec(memory_space=pltpu.VMEM)
    cells = total * RUN * SUB

    def body(*refs):
        propagate_kernel(cap, runs, row_runs, *refs)

    padded = pltpu.VMEM((total + 2 * row_runs, SUB, RUN), jnp.float32)
    return pl.pallas_call(
        body,
        in_specs=[smem] * 3 + [vmem] * 7,
        out_specs=vmem,
        out_shape=jax.ShapeDtypeStruct(recv.shape, jnp.float32),
        scratch_shapes=[padded, padded, pltpu.VMEM((total, SUB, RUN), jnp.float32)],
        cost_estimate=pl.CostEstimate(flops=100 * cells, bytes_accessed=40 * cells, transcendentals=0),
        compiler_params=pltpu.CompilerParams(vmem_limit_bytes=32 * MIB),
        name="propagate",
    )(slot, off, info, recv, idxu, idxp, wet, cx, cy, counts)


def finish_kernel(cap, runs, comps, steps, begin, end, off, idxu, recv, forced, *rest):
    if begin:
        out, total = rest
    else:
        before, _, out, total = rest
    groups = forced.shape[0] // SUB
    lane = lanes()
    step = pl.program_id(0)

    @pl.when(step == 0)
    def _():
        total[...] = jnp.zeros_like(total) if begin else before[...]

    spots = [place(off[t, 0], cap) for t in range(runs)]
    for g in range(groups):
        rows = slice(g * SUB, (g + 1) * SUB)
        done = []
        for t in range(runs):
            first, start = spots[t]
            index = rows_of(idxu, t)
            window = jnp.where(lane >= start, recv[g, first], recv[g, jnp.minimum(first + 1, cap - 1)])
            cells = lane_gather(window, jnp.bitwise_and(index, RUN - 1))
            done.append(jnp.where(index < RUN, cells, forced[rows, columns(t)]))
        for t in range(runs):
            out[rows, columns(t)] = done[t]
    for t in range(runs):
        cols = columns(t)
        added = [out[g * SUB : (g + 1) * SUB, cols] for g in range(groups)]
        while len(added) > 1:
            added = [sum(added[k : k + 2]) for k in range(0, len(added), 2)]
        total[:, cols] = total[:, cols] + added[0]

    if end:

        @pl.when(step == steps - 1)
        def _():
            mean = jnp.sum(total[...], axis=0, keepdims=True) / comps
            height = 4.0 * jnp.sqrt(mean + 1e-06)
            total[...] = jnp.broadcast_to(height, total.shape)


def finish(cap, comps, chunk, begin, end, off, idxu, recv, forced, before, out):
    points = forced.shape[1]
    runs = points // RUN
    groups = recv.shape[0]
    block_groups = 4
    steps = groups // block_groups
    base = chunk * steps
    whole = lambda i: (0, 0)
    specs = [
        pl.BlockSpec(memory_space=pltpu.SMEM),
        pl.BlockSpec((runs, RUN), whole),
        pl.BlockSpec((block_groups, cap, SUB, RUN), lambda i: (i, 0, 0, 0)),
        pl.BlockSpec((block_groups * SUB, points), lambda i: (i, 0)),
    ]
    args = [off, idxu, recv, forced]
    aliases = {}
    if not begin:
        specs += [pl.BlockSpec((SUB, points), whole), pl.BlockSpec(memory_space=pl.ANY)]
        args += [before, out]
        aliases = {5: 0}
    cells = groups * SUB * points

    def body(*refs):
        finish_kernel(cap, runs, comps, steps, begin, end, *refs)

    return pl.pallas_call(
        body,
        grid=(steps,),
        in_specs=specs,
        out_specs=[
            pl.BlockSpec((block_groups * SUB, points), lambda i: (base + i, 0)),
            pl.BlockSpec((SUB, points), whole),
        ],
        out_shape=[
            jax.ShapeDtypeStruct((comps, points), jnp.float32),
            jax.ShapeDtypeStruct((SUB, points), jnp.float32),
        ],
        input_output_aliases=aliases,
        cost_estimate=pl.CostEstimate(flops=4 * cells, bytes_accessed=12 * cells, transcendentals=0),
        compiler_params=pltpu.CompilerParams(vmem_limit_bytes=16 * MIB),
        name="finish",
    )(*args)


def packed(spectrum, wind, growth, whitecap, courant, substeps, limiter, deck, wet):
    axes = ("pt", "comp")
    comp_count = lax.axis_size("comp")
    devices = lax.axis_size("pt") * comp_count
    rank = lax.axis_index("pt") * comp_count + lax.axis_index("comp")
    comps, points = spectrum.shape
    runs = points // RUN
    total = deck.shape[0] // RUN
    row_runs = wet.shape[1] // RUN
    chunks = comps // (devices * SUB)
    small = (runs * 25 + 31) // 32

    deck = deck.reshape(total, RUN)
    wind = wind[None, :]
    limiter = limiter[None, :]
    growth = growth.reshape(comps // RUN, RUN)
    whitecap = whitecap.reshape(comps // RUN, RUN)
    forced, sent_small, sent_full, idxu, idxp, offs, own_idxu, own_idxp, own_off, ratio, need = begin(
        small, runs, row_runs, devices, rank[None].astype(jnp.int32), deck, wet, wind, limiter,
        growth, whitecap, spectrum,
    )

    def branch(cap, first):
        def run(spectrum):
            kept = [forced]
            received = [
                lax.all_to_all(
                    first.reshape(devices, cap, SUB, RUN), axes, split_axis=0, concat_axis=0, tiled=True
                )
            ]
            for chunk in range(1, chunks):
                held, sent = sources(
                    cap, chunk, devices, own_off, wind, limiter, ratio, growth, whitecap, own_idxp, spectrum
                )
                kept.append(held)
                received.append(lax.all_to_all(sent, axes, split_axis=0, concat_axis=0, tiled=True))
            slot = deck[:, 0] // RUN
            off = offs[:, 0]
            wet_runs = wet.reshape(total, RUN)
            returned = []
            for chunk in range(chunks):
                mine = (chunk * devices + rank) * SUB + jnp.arange(SUB, dtype=jnp.int32)
                cross, along = courants(mine, courant)
                counts = substeps[mine]
                info = jnp.stack(
                    [
                        jnp.where(cross[0] > 0, -row_runs, row_runs),
                        jnp.where(along[0] > 0, 1, -1),
                        jnp.max(counts),
                    ]
                ).astype(jnp.int32)
                wide = lambda v: jnp.broadcast_to(v[:, None], (SUB, RUN))
                sent = propagate(
                    cap, runs, row_runs, slot, off, info, received[chunk].reshape(devices * cap, SUB, RUN),
                    idxu, idxp, wet_runs, wide(jnp.abs(cross)), wide(jnp.abs(along)), wide(counts),
                )
                returned.append(
                    lax.all_to_all(
                        sent.reshape(devices, cap, SUB, RUN), axes, split_axis=0, concat_axis=0, tiled=True
                    )
                )
            out, sums = None, None
            for chunk in range(chunks):
                out, sums = finish(
                    cap, comps, chunk, chunk == 0, chunk == chunks - 1, own_off, own_idxu,
                    returned[chunk], kept[chunk], sums, out,
                )
            return out, sums[0]

        return run

    return lax.cond(need[0] <= small * RUN, branch(small, sent_small), branch(runs, sent_full), spectrum)


def fits(spectrum, deck, wet, devices):
    comps, points = spectrum.shape
    runs = points // RUN
    return (
        comps % (devices * SUB) == 0
        and devices % 16 == 0
        and runs % SUB == 0
        and RUN % runs == 0
        and wet.shape[0] % RUN == 0
        and deck.shape[0] % (RUN * RUN) == 0
    )


def on_device(spectrum, *rest):
    devices = lax.axis_size("pt") * lax.axis_size("comp")
    if fits(spectrum, *rest[-2:], devices):
        return packed(spectrum, *rest)
    return plain(spectrum, *rest)


def solution(mesh):
    in_specs = (
        P(None, ("pt", "comp")),
        P(("pt", "comp")),
        P(),
        P(),
        P(),
        P(),
        P(("pt", "comp")),
        P(),
        P(),
    )
    out_specs = (P(None, ("pt", "comp")), P(("pt", "comp")))
    return jax.shard_map(
        on_device, mesh=mesh, in_specs=in_specs, out_specs=out_specs, check_vma=False
    )
```

```python
import math

import jax
import jax.numpy as jnp
from jax import lax
from jax.experimental import pallas as pl
from jax.experimental.pallas import tpu as pltpu
from jax.sharding import PartitionSpec as P

DIRS = 32
MAXSUB = 8
RUN = 128
SUB = 8

rate_limit = 0.5
time_step = 0.5

FINISH_PARTS = 8
VMEM_GRANT = 60 * 1024 * 1024


def plain_sources(spectrum, wind, growth, whitecap, limiter):
    mean_energy = jnp.mean(spectrum, axis=0)
    rate = (
        wind[None, :] * growth[:, None]
        - whitecap[:, None] * (mean_energy / (1.0 + mean_energy))[None, :]
    )
    rate = jnp.where(limiter[None, :] == 1, rate_limit * jnp.tanh(rate / rate_limit), rate)
    return spectrum * jnp.exp(time_step * rate)


def plain_substep(field_grid, cross, along, wetness):
    sea = field_grid * wetness[None, :, :]
    east = jnp.roll(sea, 1, axis=2)
    west = jnp.roll(sea, -1, axis=2)
    up_column = jnp.where(along[:, None, None] > 0, east, west)
    zero_row = jnp.zeros_like(sea[:, :1, :])
    south = jnp.concatenate([zero_row, sea[:, :-1, :]], axis=1)
    north = jnp.concatenate([sea[:, 1:, :], zero_row], axis=1)
    up_row = jnp.where(cross[:, None, None] > 0, south, north)
    moved = (
        field_grid
        - jnp.abs(cross)[:, None, None] * (field_grid - up_row)
        - jnp.abs(along)[:, None, None] * (field_grid - up_column)
    )
    return jnp.where(wetness[None, :, :] > 0, moved, field_grid)


def plain(spectrum, wind, growth, whitecap, courant, substeps, limiter, deck, wet):
    forced = plain_sources(spectrum, wind, growth, whitecap, limiter)
    comp_count = lax.axis_size("comp")
    group_size = lax.axis_size("pt") * comp_count
    total_comps, point_count = forced.shape
    per_device = total_comps // group_size
    all_points = deck.shape[0]
    rows_grid, cols_grid = wet.shape
    run_count = all_points // RUN
    received = lax.all_to_all(
        forced.reshape(per_device, group_size, point_count),
        ("pt", "comp"),
        split_axis=1,
        concat_axis=1,
        tiled=True,
    )
    fields = received.reshape(per_device, run_count, RUN)
    own_rank = lax.axis_index("pt") * comp_count + lax.axis_index("comp")
    comps = jnp.arange(per_device, dtype=jnp.int32) * group_size + own_rank
    cross, along = courants(comps, courant)
    counts = substeps[comps]
    wetness = wet.astype(jnp.float32)
    slot_runs = deck.reshape(run_count, RUN)[:, 0] // RUN
    cell_runs = jnp.zeros((run_count,), jnp.int32).at[slot_runs].set(
        jnp.arange(run_count, dtype=jnp.int32)
    )
    field_grid = jnp.take(fields, cell_runs, axis=1).reshape(per_device, rows_grid, cols_grid)
    for step in range(MAXSUB):
        field_grid = jnp.where(
            step < counts[:, None, None],
            plain_substep(field_grid, cross, along, wetness),
            field_grid,
        )
    slots = jnp.take(field_grid.reshape(per_device, run_count, RUN), slot_runs, axis=1)
    back = lax.all_to_all(
        slots.reshape(per_device, group_size, point_count),
        ("pt", "comp"),
        split_axis=1,
        concat_axis=1,
        tiled=True,
    )
    arrived = back.reshape(total_comps, point_count)
    height = 4.0 * jnp.sqrt(jnp.mean(arrived, axis=0) + 1e-06)
    return (arrived, height)


def courants(comps, courant):
    angle = 2.0 * math.pi / DIRS * ((comps % DIRS).astype(jnp.float32) + 0.5)
    speed = courant[comps // DIRS]
    return speed * jnp.sin(angle), speed * jnp.cos(angle)


def lane_gather(x, idx):
    dims = lax.GatherDimensionNumbers(
        offset_dims=(),
        collapsed_slice_dims=(1,),
        start_index_map=(1,),
        operand_batching_dims=(0,),
        start_indices_batching_dims=(0,),
    )
    return lax.gather(
        x, idx[..., None], dims, slice_sizes=(1, 1), mode=lax.GatherScatterMode.PROMISE_IN_BOUNDS
    )


def lanes(rows=SUB):
    return lax.broadcasted_iota(jnp.int32, (rows, RUN), 1)


def rows_of(block, j):
    return jnp.broadcast_to(block[j : j + 1, :], (SUB, RUN))


def place(off, cap):
    first = jnp.minimum(off // RUN, cap - 1)
    return first, off - first * RUN


def columns(t):
    return slice(t * RUN, (t + 1) * RUN)


def write_stream(values, spots, lane, store, cap):
    merged = values[0]
    for t, (value, (first, start)) in enumerate(zip(values, spots)):
        if t > 0:
            before = jnp.where(first == spots[t - 1][0], merged, values[t - 1])
            merged = jnp.where(lane >= start, value, before)
        if t == len(values) - 1:
            store(jnp.minimum(first + 1, cap - 1), value)
        store(first, merged)


def force(value, wind, ratio, limited, growth, whitecap):
    rate = wind * growth - whitecap * ratio
    rate = jnp.where(limited, rate_limit * jnp.tanh(rate / rate_limit), rate)
    return value * jnp.exp(time_step * rate)


def spread(row):
    return jnp.transpose(jnp.broadcast_to(row, (RUN, RUN)))


def dot(a, b):
    return jnp.dot(a, b, preferred_element_type=jnp.float32)


def one(mask):
    return jnp.where(mask, 1.0, 0.0).astype(jnp.bfloat16)


def lay_out(wet, sea, row_runs):
    halves = wet.shape[0] // RUN
    for q in range(row_runs):
        for h in range(halves):
            k = q * halves + h
            sea[k * RUN : (k + 1) * RUN, :] = wet[h * RUN : (h + 1) * RUN, columns(q)].astype(
                jnp.float32
            ).astype(jnp.bfloat16)


def picks(slot, row_runs, halves):
    lane = lanes(slot.shape[0])
    return jnp.concatenate(
        [
            one(slot == lane * row_runs + (h * RUN * row_runs + q))
            for q in range(row_runs)
            for h in range(halves)
        ],
        axis=1,
    )


def stream_tables(wet_here, before):
    lane = lanes(wet_here.shape[0])
    wet_low = wet_here.astype(jnp.bfloat16)
    square = lambda: (lax.broadcasted_iota(jnp.int32, (RUN, RUN), 0), lanes(RUN))
    row, column = square()
    prefix = dot(wet_low, one(row < column))
    count = dot(wet_low, jnp.ones((RUN, RUN), jnp.bfloat16))
    off = dot(before, count.astype(jnp.bfloat16)).astype(jnp.int32)
    through = (prefix + wet_here).astype(jnp.int32)
    spot = jnp.bitwise_and(off + prefix.astype(jnp.int32), RUN - 1)
    idxu = jnp.where(wet_here > 0.5, spot, spot + RUN)
    nth = jnp.bitwise_and(lane - off, RUN - 1)
    at = jnp.zeros(nth.shape, jnp.int32)
    bit = RUN // 2
    while bit:
        probe = lane_gather(through, at + (bit - 1))
        at = jnp.where(probe <= nth, at + bit, at)
        bit //= 2
    return off, idxu, at


def begin_kernel(
    small, runs, row_runs, rank, deck, wet, wind, limiter, growth, whitecap, spectrum,
    sent_small, sent_full, own_idxu, own_idxp, own_off, ratio, need,
    values, packed, sea, total, grown, capped, off, in_sems, sent_sems, off_sem,
):
    comps = values.shape[0]
    slots = deck.shape[0]
    groups = packed.shape[0]
    parts = in_sems.shape[0]
    part = comps // parts

    def fetch(p):
        rows = pl.ds(p * part, part)
        return pltpu.make_async_copy(spectrum.at[rows], values.at[rows], in_sems.at[p])

    for p in range(parts):
        fetch(p).start()

    halves = wet.shape[0] // RUN
    lay_out(wet, sea, row_runs)
    ones = jnp.ones((RUN, RUN), jnp.bfloat16)

    mine = pl.ds(pl.multiple_of(rank[0] * runs, SUB), runs)
    wet_mine = dot(picks(deck[mine, :] // RUN, row_runs, halves), sea[...])
    below = lax.broadcasted_iota(jnp.int32, (runs, runs), 1) < lax.broadcasted_iota(jnp.int32, (runs, runs), 0)
    own_off[...], own_idxu[...], own_idxp[...] = stream_tables(wet_mine, one(below))
    off_copy = pltpu.make_async_copy(own_off, off, off_sem)
    off_copy.start()

    same = one(lanes(RUN) // runs == lax.broadcasted_iota(jnp.int32, (RUN, RUN), 0) // runs)
    counts = dot(sea[...], ones).astype(jnp.bfloat16)
    most = None
    for b in range(slots // RUN):
        here = dot(picks(deck[b * RUN : (b + 1) * RUN, :] // RUN, row_runs, halves), counts)
        sums = dot(same, here.astype(jnp.bfloat16))
        most = sums if most is None else jnp.maximum(most, sums)
    most = jnp.max(most).astype(jnp.int32)
    need[0] = most

    for r in range(grown.shape[0] // RUN):
        rows = slice(r * RUN, (r + 1) * RUN)
        grown[rows, :] = spread(growth[r : r + 1, :])
        capped[rows, :] = spread(whitecap[r : r + 1, :])

    for p in range(parts):
        fetch(p).wait()
        for t in range(runs):
            cols = columns(t)
            added = [values[p * part + g * SUB : p * part + (g + 1) * SUB, cols] for g in range(part // SUB)]
            while len(added) > 1:
                added = [sum(added[k : k + 2]) for k in range(0, len(added), 2)]
            total[:, cols] = added[0] if p == 0 else total[:, cols] + added[0]
    mean = jnp.sum(total[...], axis=0, keepdims=True) / comps
    ratio[...] = jnp.broadcast_to(mean / (1.0 + mean), ratio.shape)

    off_copy.wait()
    fits_small = most <= small * RUN
    cap = jnp.where(fits_small, small, runs)
    reg_lane = lanes()
    several = 8
    tall = several * SUB

    def pass_on(i, size, target):
        these = pl.ds(i * several, several)
        return pltpu.make_async_copy(packed.at[these, pl.ds(0, size)], target.at[these], sent_sems.at[i])

    def some(i, carry):
        spots = [place(off[t, 0], cap) for t in range(runs)]
        here = packed.at[pl.ds(i * several, several)]
        for g in range(several):
            rows = pl.ds(pl.multiple_of(i * tall + g * SUB, SUB), SUB)
            forced = []
            for t in range(runs):
                cols = columns(t)
                wind_t = jnp.broadcast_to(wind[:, cols], (SUB, RUN))
                limited = jnp.broadcast_to(limiter[:, cols], (SUB, RUN)) == 1
                forced.append(
                    force(values[rows, cols], wind_t, ratio[:, cols], limited, grown[rows, :], capped[rows, :])
                )
            sent = [lane_gather(forced[t], rows_of(own_idxp, t)) for t in range(runs)]

            def store(at, value, g=g):
                here[g, at] = value

            write_stream(sent, spots, reg_lane, store, cap)

        @pl.when(fits_small)
        def _():
            pass_on(i, small, sent_small).start()

        @pl.when(jnp.logical_not(fits_small))
        def _():
            pass_on(i, runs, sent_full).start()

        return carry

    lax.fori_loop(0, groups // several, some, 0)

    def drain(i, carry):
        @pl.when(fits_small)
        def _():
            pass_on(i, small, sent_small).wait()

        @pl.when(jnp.logical_not(fits_small))
        def _():
            pass_on(i, runs, sent_full).wait()

        return carry

    lax.fori_loop(0, groups // several, drain, 0)


def begin(small, runs, row_runs, groups, rank, deck, wet, wind, limiter, growth, whitecap, spectrum):
    comps, points = spectrum.shape
    slots = deck.shape[0]
    block = groups * SUB
    parts = 8
    smem = pl.BlockSpec(memory_space=pltpu.SMEM)
    vmem = pl.BlockSpec(memory_space=pltpu.VMEM)
    far = pl.BlockSpec(memory_space=pltpu.HBM)
    cells = comps * points
    f32 = lambda *shape: jax.ShapeDtypeStruct(shape, jnp.float32)
    i32 = lambda *shape: jax.ShapeDtypeStruct(shape, jnp.int32)

    def body(*refs):
        begin_kernel(small, runs, row_runs, *refs)

    return pl.pallas_call(
        body,
        in_specs=[smem, vmem, vmem, vmem, vmem, vmem, vmem, far],
        out_specs=[far] * 2 + [vmem] * 4 + [smem],
        out_shape=[
            f32(groups, small, SUB, RUN),
            f32(groups, runs, SUB, RUN),
            i32(runs, RUN),
            i32(runs, RUN),
            i32(runs, RUN),
            f32(SUB, points),
            i32(1),
        ],
        scratch_shapes=[
            pltpu.VMEM((comps, points), jnp.float32),
            pltpu.VMEM((groups, runs, SUB, RUN), jnp.float32),
            pltpu.VMEM((slots, RUN), jnp.bfloat16),
            pltpu.VMEM((SUB, points), jnp.float32),
            pltpu.VMEM((block, RUN), jnp.float32),
            pltpu.VMEM((block, RUN), jnp.float32),
            pltpu.SMEM((runs, RUN), jnp.int32),
            pltpu.SemaphoreType.DMA((parts,)),
            pltpu.SemaphoreType.DMA((groups,)),
            pltpu.SemaphoreType.DMA,
        ],
        cost_estimate=pl.CostEstimate(flops=10 * cells, bytes_accessed=10 * cells, transcendentals=cells),
        compiler_params=pltpu.CompilerParams(vmem_limit_bytes=VMEM_GRANT),
        name="begin",
    )(rank, deck, wet, wind, limiter, growth, whitecap, spectrum)


def tables_kernel(runs, row_runs, deck, wet, idxu, idxp, off, slot, sea):
    lay_out(wet, sea, row_runs)
    row = lax.broadcasted_iota(jnp.int32, (RUN, RUN), 0)
    lane = lanes(RUN)
    before = one((lane < row) & (lane // runs == row // runs))
    halves = wet.shape[0] // RUN

    def block(b, carry):
        here = pl.ds(pl.multiple_of(b * RUN, RUN), RUN)
        slot_b = deck[here, :] // RUN
        off_b, idxu[here, :], idxp[here, :] = stream_tables(
            dot(picks(slot_b, row_runs, halves), sea[...]), before
        )
        off[pl.ds(b, 1), :] = jnp.transpose(off_b)[:1, :]
        slot[pl.ds(b, 1), :] = jnp.transpose(slot_b)[:1, :]
        return carry

    lax.fori_loop(0, deck.shape[0] // RUN, block, 0)


def tables(runs, row_runs, deck, wet):
    slots = deck.shape[0]
    vmem = pl.BlockSpec(memory_space=pltpu.VMEM)
    i32 = lambda *shape: jax.ShapeDtypeStruct(shape, jnp.int32)

    def body(*refs):
        tables_kernel(runs, row_runs, *refs)

    return pl.pallas_call(
        body,
        in_specs=[vmem, vmem],
        out_specs=[vmem] * 4,
        out_shape=[i32(slots, RUN), i32(slots, RUN), i32(slots // RUN, RUN), i32(slots // RUN, RUN)],
        scratch_shapes=[pltpu.VMEM((slots, RUN), jnp.bfloat16)],
        cost_estimate=pl.CostEstimate(flops=2 * slots * slots * RUN, bytes_accessed=16 * slots * RUN, transcendentals=0),
        compiler_params=pltpu.CompilerParams(vmem_limit_bytes=VMEM_GRANT),
        name="tables",
    )(deck, wet)


def source_kernel(cap, runs, off, wind, limiter, ratio, growth, whitecap, idxp, spectrum, forced, *packed):
    groups = spectrum.shape[0] // SUB
    lane = lanes()
    block = groups * SUB
    grown = spread(growth[...].reshape(1, RUN))
    capped = spread(whitecap[...].reshape(1, RUN))
    spots = [place(off[t, 0], cap) for t in range(runs)]
    for g in range(groups):
        rows = slice(g * SUB, (g + 1) * SUB)
        values = []
        for t in range(runs):
            cols = columns(t)
            wind_t = jnp.broadcast_to(wind[:, cols], (SUB, RUN))
            limited = jnp.broadcast_to(limiter[:, cols], (SUB, RUN)) == 1
            values.append(
                force(spectrum[rows, cols], wind_t, ratio[:, cols], limited, grown[rows, :], capped[rows, :])
            )
        for t in range(runs):
            forced[rows, columns(t)] = values[t]
        if packed:
            sent = [lane_gather(values[t], rows_of(idxp, t)) for t in range(runs)]

            def store(at, value, g=g):
                packed[0][g, at] = value

            write_stream(sent, spots, lane, store, cap)


def sources(cap, chunk, groups, pack, off, wind, limiter, ratio, growth, whitecap, idxp, spectrum):
    points = spectrum.shape[1]
    runs = points // RUN
    block = RUN
    block_groups = block // SUB
    steps = groups // block_groups
    base = chunk * steps
    whole = lambda i: (0, 0)
    cells = groups * SUB * points

    def body(*refs):
        source_kernel(cap, runs, *refs)

    return pl.pallas_call(
        body,
        grid=(steps,),
        in_specs=[
            pl.BlockSpec(memory_space=pltpu.SMEM),
            pl.BlockSpec((1, points), whole),
            pl.BlockSpec((1, points), whole),
            pl.BlockSpec((SUB, points), whole),
            pl.BlockSpec((1, 1, RUN), lambda i: (base + i, 0, 0)),
            pl.BlockSpec((1, 1, RUN), lambda i: (base + i, 0, 0)),
            pl.BlockSpec((runs, RUN), whole),
            pl.BlockSpec((block, points), lambda i: (base + i, 0)),
        ],
        out_specs=[
            pl.BlockSpec((block, points), lambda i: (i, 0)),
            pl.BlockSpec((block_groups, cap, SUB, RUN), lambda i: (i, 0, 0, 0)),
        ][: 1 + pack],
        out_shape=[
            pltpu.HBM((groups * SUB, points), jnp.float32),
            pltpu.HBM((groups, cap, SUB, RUN), jnp.float32),
        ][: 1 + pack],
        cost_estimate=pl.CostEstimate(flops=10 * cells, bytes_accessed=12 * cells, transcendentals=2 * cells),
        compiler_params=pltpu.CompilerParams(vmem_limit_bytes=VMEM_GRANT),
        name="sources",
    )(off, wind, limiter, ratio, growth[:, None, :], whitecap[:, None, :], idxp, spectrum)


def propagate_kernel(
    cap, runs, row_runs, slot, off, info, recv, idxu, idxp, wet, cx, cy, counts, sent, field, other, wide
):
    total = slot.shape[0]
    lane = lanes()
    blank = jnp.zeros((SUB, RUN), jnp.float32)
    for ref in (field, other):
        for q in range(row_runs):
            ref[q] = blank
            ref[row_runs + total + q] = blank

    span = 4 * SUB

    def spread_wet(i, carry):
        t0 = pl.multiple_of(i * span, SUB)
        block = wet[pl.ds(t0, span), :].astype(jnp.float32)
        for j in range(span):
            wide[t0 + j] = rows_of(block, j)
        return carry

    lax.fori_loop(0, total // span, spread_wet, 0)

    def unpack(i, carry):
        t0 = pl.multiple_of(i * runs, SUB)
        base = i * cap
        indices = idxu[pl.ds(t0, runs), :]
        done = []
        for j in range(runs):
            first, start = place(off[t0 + j], cap)
            second = jnp.minimum(first + 1, cap - 1)
            window = jnp.where(lane >= start, recv[base + first], recv[base + second])
            index = rows_of(indices, j)
            cells = lane_gather(window, jnp.bitwise_and(index, RUN - 1))
            done.append(jnp.where(index < RUN, cells, 0.0))
        for j in range(runs):
            field[row_runs + slot[t0 + j]] = done[j]
        return carry

    lax.fori_loop(0, total // runs, unpack, 0)

    up_row = info[0]
    last = info[2]
    block = 32 * row_runs

    def run_steps(eastward):
        edge = lane == (0 if eastward else RUN - 1)
        shift = 1 if eastward else RUN - 1

        def step(n, src, dst):
            on = n < counts[...]
            b = jnp.where(on, cx[...], 0.0)
            c = jnp.where(on, cy[...], 0.0)
            a = 1.0 - b - c

            def rows(i, inner):
                t0 = i * block
                here = src[pl.ds(row_runs + t0, block)]
                up_x = src[pl.ds(row_runs + t0 + up_row, block)]
                sea = wide[pl.ds(t0, block)]
                rolled = [pltpu.roll(here[k], shift, 1) for k in range(block)]
                out = []
                for k in range(block):
                    q = k % row_runs
                    near = rolled[k - q + (q - 1 if eastward else q + 1) % row_runs]
                    up_y = jnp.where(edge, near, rolled[k])
                    out.append(sea[k] * (a * here[k] + b * up_x[k] + c * up_y))
                dst[pl.ds(row_runs + t0, block)] = jnp.stack(out)
                return inner

            lax.fori_loop(0, total // block, rows, 0)

        def pair(m, carry):
            step(2 * m, field, other)
            step(2 * m + 1, other, field)
            return carry

        lax.fori_loop(0, (last + 1) // 2, pair, 0)

    @pl.when(info[1] > 0)
    def _():
        run_steps(True)

    @pl.when(info[1] <= 0)
    def _():
        run_steps(False)

    def pack(i, carry):
        t0 = pl.multiple_of(i * runs, SUB)
        indices = idxp[pl.ds(t0, runs), :]
        picked = [
            lane_gather(field[row_runs + slot[t0 + j]], rows_of(indices, j)) for j in range(runs)
        ]
        spots = [place(off[t0 + j], cap) for j in range(runs)]

        def store(at, value):
            sent[i * cap + at] = value

        write_stream(picked, spots, lane, store, cap)
        return carry

    lax.fori_loop(0, total // runs, pack, 0)


def propagate(cap, runs, row_runs, slot, off, info, recv, idxu, idxp, wet, cx, cy, counts):
    total = slot.shape[0]
    smem = pl.BlockSpec(memory_space=pltpu.SMEM)
    vmem = pl.BlockSpec(memory_space=pltpu.VMEM)
    cells = total * RUN * SUB

    def body(*refs):
        propagate_kernel(cap, runs, row_runs, *refs)

    padded = pltpu.VMEM((total + 2 * row_runs, SUB, RUN), jnp.float32)
    return pl.pallas_call(
        body,
        in_specs=[smem] * 3 + [vmem] * 7,
        out_specs=vmem,
        out_shape=jax.ShapeDtypeStruct(recv.shape, jnp.float32),
        scratch_shapes=[padded, padded, pltpu.VMEM((total, SUB, RUN), jnp.float32)],
        cost_estimate=pl.CostEstimate(flops=100 * cells, bytes_accessed=40 * cells, transcendentals=0),
        compiler_params=pltpu.CompilerParams(vmem_limit_bytes=VMEM_GRANT),
        name="propagate",
    )(slot, off, info, recv, idxu, idxp, wet, cx, cy, counts)


def finish_kernel(cap, runs, comps, base, begin, end, off, idxu, recv, forced, *rest):
    if begin:
        out, total, streams, values, stream_sems, value_sems, out_sems = rest
    else:
        before, _, out, total, streams, values, stream_sems, value_sems, out_sems = rest
    lane = lanes()
    parts = stream_sems.shape[0]
    groups = recv.shape[0] // parts
    tall = groups * SUB

    def arrive(p):
        some = pl.ds(p * groups, groups)
        return pltpu.make_async_copy(recv.at[some], streams.at[some], stream_sems.at[p])

    def bring(p):
        rows = pl.ds(pl.multiple_of(p * tall, SUB), tall)
        return pltpu.make_async_copy(forced.at[rows], values.at[rows], value_sems.at[p])

    def leave(p):
        rows = pl.ds(pl.multiple_of(p * tall, SUB), tall)
        there = pl.ds(pl.multiple_of(base + p * tall, SUB), tall)
        return pltpu.make_async_copy(values.at[rows], out.at[there], out_sems.at[p])

    for p in range(parts):
        arrive(p).start()
        bring(p).start()
    total[...] = jnp.zeros_like(total) if begin else before[...]

    def some(p, carry):
        arrive(p).wait()
        bring(p).wait()
        here = streams.at[pl.ds(p * groups, groups)]
        block = values.at[pl.ds(pl.multiple_of(p * tall, SUB), tall)]
        rows = [slice(g * SUB, (g + 1) * SUB) for g in range(groups)]
        for t0 in range(0, runs, SUB):
            done = []
            for t in range(t0, t0 + SUB):
                first, start = place(off[t, 0], cap)
                second = jnp.minimum(first + 1, cap - 1)
                index = rows_of(idxu, t)
                sea = index < RUN
                index = jnp.bitwise_and(index, RUN - 1)
                lower = lane >= start
                cells = [
                    lane_gather(jnp.where(lower, here[g, first], here[g, second]), index) for g in range(groups)
                ]
                done.append([jnp.where(sea, cells[g], block[rows[g], columns(t)]) for g in range(groups)])
            for k, settled in enumerate(done):
                cols = columns(t0 + k)
                added = total[:, cols]
                for g in range(groups):
                    block[rows[g], cols] = settled[g]
                    added = added + settled[g]
                total[:, cols] = added
        leave(p).start()
        return carry

    lax.fori_loop(0, parts, some, 0)
    if end:
        mean = jnp.sum(total[...], axis=0, keepdims=True) / comps
        height = 4.0 * jnp.sqrt(mean + 1e-06)
        total[...] = jnp.broadcast_to(height, total.shape)

    def drain(p, carry):
        leave(p).wait()
        return carry

    lax.fori_loop(0, parts, drain, 0)


def finish(cap, comps, chunk, begin, end, off, idxu, recv, forced, before, out):
    block, points = forced.shape
    runs = points // RUN
    parts = FINISH_PARTS
    smem = pl.BlockSpec(memory_space=pltpu.SMEM)
    whole = lambda *shape: pl.BlockSpec(shape, lambda i: (0, 0))
    far = pl.BlockSpec(memory_space=pltpu.HBM)
    specs = [smem, whole(runs, RUN), far, far]
    args = [off, idxu, recv, forced]
    aliases = {}
    if not begin:
        specs += [whole(SUB, points), far]
        args += [before, out]
        aliases = {5: 0}
    cells = block * points

    def body(*refs):
        finish_kernel(cap, runs, comps, chunk * block, begin, end, *refs)

    return pl.pallas_call(
        body,
        grid=(1,),
        in_specs=specs,
        out_specs=[far, whole(SUB, points)],
        out_shape=[
            jax.ShapeDtypeStruct((comps, points), jnp.float32),
            jax.ShapeDtypeStruct((SUB, points), jnp.float32),
        ],
        scratch_shapes=[
            pltpu.VMEM(recv.shape, jnp.float32),
            pltpu.VMEM((block, points), jnp.float32),
            pltpu.SemaphoreType.DMA((parts,)),
            pltpu.SemaphoreType.DMA((parts,)),
            pltpu.SemaphoreType.DMA((parts,)),
        ],
        input_output_aliases=aliases,
        cost_estimate=pl.CostEstimate(flops=4 * cells, bytes_accessed=12 * cells, transcendentals=0),
        compiler_params=pltpu.CompilerParams(vmem_limit_bytes=VMEM_GRANT),
        name="finish",
    )(*args)


def packed(spectrum, wind, growth, whitecap, courant, substeps, limiter, deck, wet):
    axes = ("pt", "comp")
    comp_count = lax.axis_size("comp")
    devices = lax.axis_size("pt") * comp_count
    rank = lax.axis_index("pt") * comp_count + lax.axis_index("comp")
    comps, points = spectrum.shape
    runs = points // RUN
    total = deck.shape[0] // RUN
    row_runs = wet.shape[1] // RUN
    chunks = comps // (devices * SUB)
    small = (runs * 25 + 31) // 32

    deck = deck.reshape(total, RUN)
    wind = wind[None, :]
    limiter = limiter[None, :]
    growth = growth.reshape(comps // RUN, RUN)
    whitecap = whitecap.reshape(comps // RUN, RUN)
    sent_small, sent_full, own_idxu, own_idxp, own_off, ratio, need = begin(
        small, runs, row_runs, devices, rank[None].astype(jnp.int32), deck, wet, wind, limiter,
        growth, whitecap, spectrum,
    )

    def branch(cap, first):
        def run(spectrum):
            kept = []
            received = []
            for chunk in range(chunks):
                held, *sent = sources(
                    cap, chunk, devices, chunk > 0, own_off, wind, limiter, ratio, growth, whitecap,
                    own_idxp, spectrum,
                )
                kept.append(held)
                sent = sent[0] if sent else first
                received.append(lax.all_to_all(sent, axes, split_axis=0, concat_axis=0, tiled=True))
            idxu, idxp, off, slot = tables(runs, row_runs, deck, wet)
            off, slot = off.reshape(total), slot.reshape(total)
            wet_runs = wet.reshape(total, RUN)
            returned = []
            for chunk in range(chunks):
                mine = (chunk * devices + rank) * SUB + jnp.arange(SUB, dtype=jnp.int32)
                cross, along = courants(mine, courant)
                counts = substeps[mine]
                info = jnp.stack(
                    [
                        jnp.where(cross[0] > 0, -row_runs, row_runs),
                        jnp.where(along[0] > 0, 1, -1),
                        jnp.max(counts),
                    ]
                ).astype(jnp.int32)
                wide = lambda v: jnp.broadcast_to(v[:, None], (SUB, RUN))
                sent = propagate(
                    cap, runs, row_runs, slot, off, info, received[chunk].reshape(devices * cap, SUB, RUN),
                    idxu, idxp, wet_runs, wide(jnp.abs(cross)), wide(jnp.abs(along)), wide(counts),
                )
                returned.append(
                    lax.all_to_all(
                        sent.reshape(devices, cap, SUB, RUN), axes, split_axis=0, concat_axis=0, tiled=True
                    )
                )
            out, sums = None, None
            for chunk in range(chunks):
                out, sums = finish(
                    cap, comps, chunk, chunk == 0, chunk == chunks - 1, own_off, own_idxu,
                    returned[chunk], kept[chunk], sums, out,
                )
            return out, sums[0]

        return run

    return lax.cond(need[0] <= small * RUN, branch(small, sent_small), branch(runs, sent_full), spectrum)


def fits(spectrum, deck, wet, devices):
    comps, points = spectrum.shape
    runs = points // RUN
    return (
        comps % (devices * SUB) == 0
        and devices % 16 == 0
        and runs % SUB == 0
        and RUN % runs == 0
        and wet.shape[0] % RUN == 0
        and deck.shape[0] % (RUN * RUN) == 0
    )


def on_device(spectrum, *rest):
    devices = lax.axis_size("pt") * lax.axis_size("comp")
    if fits(spectrum, *rest[-2:], devices):
        return packed(spectrum, *rest)
    return plain(spectrum, *rest)


def solution(mesh):
    in_specs = (
        P(None, ("pt", "comp")),
        P(("pt", "comp")),
        P(),
        P(),
        P(),
        P(),
        P(("pt", "comp")),
        P(),
        P(),
    )
    out_specs = (P(None, ("pt", "comp")), P(("pt", "comp")))
    return jax.shard_map(
        on_device, mesh=mesh, in_specs=in_specs, out_specs=out_specs, check_vma=False
    )
```

```python
import math

import jax
import jax.numpy as jnp
from jax import lax
from jax.experimental import pallas as pl
from jax.experimental.pallas import tpu as pltpu
from jax.sharding import PartitionSpec as P

DIRS = 32
QUADRANTS = 4
MAXSUB = 8
RUN = 128
SUB = 8

rate_limit = 0.5
time_step = 0.5

FLOWS, FLOWS_AND_STAYS, STAYS, DRY = range(4)

VMEM_GRANT = 62 * 1024 * 1024


def plain_sources(spectrum, wind, growth, whitecap, limiter):
    mean_energy = jnp.mean(spectrum, axis=0)
    rate = (
        wind[None, :] * growth[:, None]
        - whitecap[:, None] * (mean_energy / (1.0 + mean_energy))[None, :]
    )
    rate = jnp.where(limiter[None, :] == 1, rate_limit * jnp.tanh(rate / rate_limit), rate)
    return spectrum * jnp.exp(time_step * rate)


def plain_substep(field_grid, cross, along, wetness):
    sea = field_grid * wetness[None, :, :]
    east = jnp.roll(sea, 1, axis=2)
    west = jnp.roll(sea, -1, axis=2)
    up_column = jnp.where(along[:, None, None] > 0, east, west)
    zero_row = jnp.zeros_like(sea[:, :1, :])
    south = jnp.concatenate([zero_row, sea[:, :-1, :]], axis=1)
    north = jnp.concatenate([sea[:, 1:, :], zero_row], axis=1)
    up_row = jnp.where(cross[:, None, None] > 0, south, north)
    moved = (
        field_grid
        - jnp.abs(cross)[:, None, None] * (field_grid - up_row)
        - jnp.abs(along)[:, None, None] * (field_grid - up_column)
    )
    return jnp.where(wetness[None, :, :] > 0, moved, field_grid)


def plain(spectrum, wind, growth, whitecap, courant, substeps, limiter, deck, wet):
    forced = plain_sources(spectrum, wind, growth, whitecap, limiter)
    comp_count = lax.axis_size("comp")
    group_size = lax.axis_size("pt") * comp_count
    total_comps, point_count = forced.shape
    per_device = total_comps // group_size
    all_points = deck.shape[0]
    rows_grid, cols_grid = wet.shape
    run_count = all_points // RUN
    received = lax.all_to_all(
        forced.reshape(per_device, group_size, point_count),
        ("pt", "comp"),
        split_axis=1,
        concat_axis=1,
        tiled=True,
    )
    fields = received.reshape(per_device, run_count, RUN)
    own_rank = lax.axis_index("pt") * comp_count + lax.axis_index("comp")
    comps = jnp.arange(per_device, dtype=jnp.int32) * group_size + own_rank
    cross, along = courants(comps, courant)
    counts = substeps[comps]
    wetness = wet.astype(jnp.float32)
    slot_runs = deck.reshape(run_count, RUN)[:, 0] // RUN
    cell_runs = jnp.zeros((run_count,), jnp.int32).at[slot_runs].set(
        jnp.arange(run_count, dtype=jnp.int32)
    )
    field_grid = jnp.take(fields, cell_runs, axis=1).reshape(per_device, rows_grid, cols_grid)
    for step in range(MAXSUB):
        field_grid = jnp.where(
            step < counts[:, None, None],
            plain_substep(field_grid, cross, along, wetness),
            field_grid,
        )
    slots = jnp.take(field_grid.reshape(per_device, run_count, RUN), slot_runs, axis=1)
    back = lax.all_to_all(
        slots.reshape(per_device, group_size, point_count),
        ("pt", "comp"),
        split_axis=1,
        concat_axis=1,
        tiled=True,
    )
    arrived = back.reshape(total_comps, point_count)
    height = 4.0 * jnp.sqrt(jnp.mean(arrived, axis=0) + 1e-06)
    return (arrived, height)


def courants(comps, courant):
    angle = 2.0 * math.pi / DIRS * ((comps % DIRS).astype(jnp.float32) + 0.5)
    speed = courant[comps // DIRS]
    return speed * jnp.sin(angle), speed * jnp.cos(angle)


def lane_gather(x, idx):
    dims = lax.GatherDimensionNumbers(
        offset_dims=(),
        collapsed_slice_dims=(1,),
        start_index_map=(1,),
        operand_batching_dims=(0,),
        start_indices_batching_dims=(0,),
    )
    return lax.gather(
        x, idx[..., None], dims, slice_sizes=(1, 1), mode=lax.GatherScatterMode.PROMISE_IN_BOUNDS
    )


def lanes(rows=SUB):
    return lax.broadcasted_iota(jnp.int32, (rows, RUN), 1)


def rows_of(block, j):
    return jnp.broadcast_to(block[j : j + 1, :], (SUB, RUN))


def split(off):
    first = lax.shift_right_logical(off, RUN.bit_length() - 1)
    return first, off - first * RUN


def place(off, cap):
    first = jnp.minimum(split(off)[0], cap - 1)
    return first, off - first * RUN


def place_all(off, q, runs, cap):
    return [place(off[q * runs + t, 0], cap) for t in range(runs)]


def columns(t):
    return slice(t * RUN, (t + 1) * RUN)


def write_stream(values, spots, lane, store, cap):
    merged = values[0]
    for t, (value, (first, start)) in enumerate(zip(values, spots)):
        if t > 0:
            before = jnp.where(first == spots[t - 1][0], merged, values[t - 1])
            merged = jnp.where(lane >= start, value, before)
        if t == len(values) - 1:
            store(jnp.minimum(first + 1, cap - 1), value)
        store(first, merged)


def force(value, wind, ratio, limited, growth, whitecap):
    rate = wind * growth - whitecap * ratio
    rate = jnp.where(limited, rate_limit * jnp.tanh(rate / rate_limit), rate)
    return value * jnp.exp(time_step * rate)


def spread(row):
    return jnp.transpose(jnp.broadcast_to(row, (RUN, RUN)))


def dot(a, b):
    return jnp.dot(a, b, preferred_element_type=jnp.float32)


def one(mask):
    return jnp.where(mask, 1.0, 0.0).astype(jnp.bfloat16)


def neighbours(wet):
    rows, cols = wet.shape
    row = lax.broadcasted_iota(jnp.int32, wet.shape, 0)
    north = jnp.where(row < rows - 1, pltpu.roll(wet, rows - 1, 0), 0.0)
    south = jnp.where(row > 0, pltpu.roll(wet, 1, 0), 0.0)
    return north, south, pltpu.roll(wet, cols - 1, 1), pltpu.roll(wet, 1, 1)


def flowing(wet):
    north, south, east, west = neighbours(wet)
    return [
        wet * jnp.maximum(along, across)
        for along, across in ((north, east), (north, west), (south, west), (south, east))
    ]


def lay_out(mask, sea, column, row_runs):
    halves = mask.shape[0] // RUN
    mask = mask.astype(jnp.bfloat16)
    for q in range(row_runs):
        for h in range(halves):
            k = q * halves + h
            sea[k * RUN : (k + 1) * RUN, columns(column)] = mask[h * RUN : (h + 1) * RUN, columns(q)]


def picks(slot, row_runs, halves):
    lane = lanes(slot.shape[0])
    return jnp.concatenate(
        [
            one(slot == lane * row_runs + (h * RUN * row_runs + q))
            for q in range(row_runs)
            for h in range(halves)
        ],
        axis=1,
    )


def stream_tables(wet_here, before, inverse=True):
    lane = lanes(wet_here.shape[0])
    wet_low = wet_here.astype(jnp.bfloat16)
    square = lambda: (lax.broadcasted_iota(jnp.int32, (RUN, RUN), 0), lanes(RUN))
    row, column = square()
    prefix = dot(wet_low, one(row < column))
    count = dot(wet_low, jnp.ones((RUN, RUN), jnp.bfloat16))
    off = dot(before, count.astype(jnp.bfloat16)).astype(jnp.int32)
    through = (prefix + wet_here).astype(jnp.int32)
    spot = jnp.bitwise_and(off + prefix.astype(jnp.int32), RUN - 1)
    idxu = jnp.where(wet_here > 0.5, spot, spot + RUN)
    nth = jnp.bitwise_and(lane - off, RUN - 1)
    at = jnp.zeros(nth.shape, jnp.int32)
    bit = RUN // 2 if inverse else 0
    while bit:
        probe = lane_gather(through, at + (bit - 1))
        at = jnp.where(probe <= nth, at + bit, at)
        bit //= 2
    return off, idxu, at


def begin_kernel(
    small, runs, row_runs, rank, deck, wet, wind, limiter, growth, whitecap, spectrum,
    sent_small, sent_full, own_code, own_idxp, own_off, ratio, need,
    values, packed, sea, total, grown, capped, off, in_sems, sent_sems, off_sem,
):
    comps = values.shape[0]
    slots = deck.shape[0]
    groups = packed.shape[1] * QUADRANTS
    parts = in_sems.shape[0]
    part = comps // parts

    def fetch(p):
        rows = pl.ds(p * part, part)
        return pltpu.make_async_copy(spectrum.at[rows], values.at[rows], in_sems.at[p])

    for p in range(parts):
        fetch(p).start()

    halves = wet.shape[0] // RUN
    wet_f = wet[...].astype(jnp.float32)
    for k, mask in enumerate(flowing(wet_f) + [wet_f]):
        lay_out(mask, sea, k, row_runs)

    mine = pl.ds(pl.multiple_of(rank[0] * runs, SUB), runs)
    found = dot(picks(deck[mine, :] // RUN, row_runs, halves), sea[...])
    lane = lanes(RUN)
    row = lax.broadcasted_iota(jnp.int32, (RUN, RUN), 0)
    same = lane // runs == row // runs
    masks = jnp.concatenate([found[:, columns(q)] for q in range(QUADRANTS)], axis=0)
    own_off[...], idxu, own_idxp[...] = stream_tables(masks, one(same & (lane < row)))
    land = found[:, columns(QUADRANTS)] < 0.5
    for q in range(QUADRANTS):
        near = slice(q * runs, (q + 1) * runs)
        back = (q + 2) % QUADRANTS
        there = idxu[back * runs : (back + 1) * runs, :]
        comes = there < RUN
        goes = idxu[near, :] < RUN
        kind = jnp.where(comes, jnp.where(goes, FLOWS, FLOWS_AND_STAYS), jnp.where(land, DRY, STAYS))
        own_code[near, :] = jnp.bitwise_and(there, RUN - 1) + RUN * kind
    off_copy = pltpu.make_async_copy(own_off, off, off_sem)
    off_copy.start()

    wide = (QUADRANTS * RUN, RUN)
    which = lax.broadcasted_iota(jnp.int32, wide, 0) // RUN == lanes(wide[0]) // (RUN // QUADRANTS)
    counts = dot(sea[:, : QUADRANTS * RUN], one(which)).astype(jnp.bfloat16)
    most = None
    for b in range(slots // RUN):
        here = dot(picks(deck[b * RUN : (b + 1) * RUN, :] // RUN, row_runs, halves), counts)
        sums = dot(one(same), here.astype(jnp.bfloat16))
        most = sums if most is None else jnp.maximum(most, sums)
    most = jnp.max(most).astype(jnp.int32)
    need[0] = most

    for r in range(grown.shape[0] // RUN):
        rows = slice(r * RUN, (r + 1) * RUN)
        grown[rows, :] = spread(growth[r : r + 1, :])
        capped[rows, :] = spread(whitecap[r : r + 1, :])

    for p in range(parts):
        fetch(p).wait()
        for t in range(runs):
            cols = columns(t)
            added = [values[p * part + g * SUB : p * part + (g + 1) * SUB, cols] for g in range(part // SUB)]
            while len(added) > 1:
                added = [sum(added[k : k + 2]) for k in range(0, len(added), 2)]
            total[:, cols] = added[0] if p == 0 else total[:, cols] + added[0]
    mean = jnp.sum(total[...], axis=0, keepdims=True) / comps
    ratio[...] = jnp.broadcast_to(mean / (1.0 + mean), ratio.shape)

    off_copy.wait()
    fits_small = most <= small * RUN
    reg_lane = lanes()
    per = groups // QUADRANTS

    def pass_on(q, size, target):
        return pltpu.make_async_copy(packed.at[q, :, pl.ds(0, size)], target.at[:, q], sent_sems.at[q])

    for q in range(QUADRANTS):
        index = [slice(g * SUB, (g + 1) * SUB) for g in range(q, groups, QUADRANTS)]
        stream = packed.at[q]
        merged, last = [None] * per, [None] * per
        first_before = None
        for t in range(runs):
            cols = columns(t)
            wind_t = jnp.broadcast_to(wind[:, cols], (SUB, RUN))
            limited = jnp.broadcast_to(limiter[:, cols], (SUB, RUN)) == 1
            ratio_t = ratio[:, cols]
            picked = rows_of(own_idxp, q * runs + t)
            offset = off[q * runs + t, 0]
            first, start = split(offset)
            taken = reg_lane >= start
            for m, rows in enumerate(index):
                value = force(values[rows, cols], wind_t, ratio_t, limited, grown[rows, :], capped[rows, :])
                value = lane_gather(value, picked)
                if t == 0:
                    merged[m] = value
                else:
                    before = jnp.where(first == first_before, merged[m], last[m])
                    merged[m] = jnp.where(taken, value, before)
                last[m] = value
                if t == runs - 1:
                    stream[m, first + 1] = value
                stream[m, first] = merged[m]
            first_before = first

        @pl.when(fits_small)
        def _(q=q):
            pass_on(q, small, sent_small).start()

        @pl.when(jnp.logical_not(fits_small))
        def _(q=q):
            pass_on(q, runs, sent_full).start()

    for q in range(QUADRANTS):

        @pl.when(fits_small)
        def _(q=q):
            pass_on(q, small, sent_small).wait()

        @pl.when(jnp.logical_not(fits_small))
        def _(q=q):
            pass_on(q, runs, sent_full).wait()


def begin(small, runs, row_runs, groups, rank, deck, wet, wind, limiter, growth, whitecap, spectrum):
    comps, points = spectrum.shape
    slots = deck.shape[0]
    block = groups * SUB
    parts = 8
    smem = pl.BlockSpec(memory_space=pltpu.SMEM)
    vmem = pl.BlockSpec(memory_space=pltpu.VMEM)
    far = pl.BlockSpec(memory_space=pltpu.HBM)
    cells = comps * points
    f32 = lambda *shape: jax.ShapeDtypeStruct(shape, jnp.float32)
    i32 = lambda *shape: jax.ShapeDtypeStruct(shape, jnp.int32)

    def body(*refs):
        begin_kernel(small, runs, row_runs, *refs)

    return pl.pallas_call(
        body,
        in_specs=[smem, vmem, vmem, vmem, vmem, vmem, vmem, far],
        out_specs=[far] * 2 + [vmem] * 4 + [smem],
        out_shape=[
            f32(groups // QUADRANTS, QUADRANTS, small, SUB, RUN),
            f32(groups // QUADRANTS, QUADRANTS, runs, SUB, RUN),
            i32(QUADRANTS * runs, RUN),
            i32(QUADRANTS * runs, RUN),
            i32(QUADRANTS * runs, RUN),
            f32(SUB, points),
            i32(1),
        ],
        scratch_shapes=[
            pltpu.VMEM((comps, points), jnp.float32),
            pltpu.VMEM((QUADRANTS, groups // QUADRANTS, runs + 1, SUB, RUN), jnp.float32),
            pltpu.VMEM((slots, (QUADRANTS + 1) * RUN), jnp.bfloat16),
            pltpu.VMEM((SUB, points), jnp.float32),
            pltpu.VMEM((block, RUN), jnp.float32),
            pltpu.VMEM((block, RUN), jnp.float32),
            pltpu.SMEM((QUADRANTS * runs, RUN), jnp.int32),
            pltpu.SemaphoreType.DMA((parts,)),
            pltpu.SemaphoreType.DMA((QUADRANTS,)),
            pltpu.SemaphoreType.DMA,
        ],
        cost_estimate=pl.CostEstimate(flops=10 * cells, bytes_accessed=10 * cells, transcendentals=cells),
        compiler_params=pltpu.CompilerParams(vmem_limit_bytes=VMEM_GRANT),
        name="begin",
    )(rank, deck, wet, wind, limiter, growth, whitecap, spectrum)


def tables_kernel(runs, row_runs, info, deck, wet, idxu, idxp, off_in, off_out, slot, sea):
    wet_f = wet[...].astype(jnp.float32)
    north, south, east, west = neighbours(wet_f)
    from_south, from_west = info[0] < 0, info[1] > 0
    ahead = jnp.maximum(jnp.where(from_south, north, south), jnp.where(from_west, east, west))
    behind = jnp.maximum(jnp.where(from_south, south, north), jnp.where(from_west, west, east))
    lay_out(wet_f * ahead, sea, 0, row_runs)
    lay_out(wet_f * behind, sea, 1, row_runs)
    row = lax.broadcasted_iota(jnp.int32, (RUN, RUN), 0)
    lane = lanes(RUN)
    before = one((lane < row) & (lane // runs == row // runs))
    halves = wet.shape[0] // RUN

    def block(b, carry):
        here = pl.ds(pl.multiple_of(b * RUN, RUN), RUN)
        slot_b = deck[here, :] // RUN
        found = dot(picks(slot_b, row_runs, halves), sea[...])
        off_b, idxu[here, :], _ = stream_tables(found[:, columns(0)], before, False)
        off_in[pl.ds(b, 1), :] = jnp.transpose(off_b)[:1, :]
        off_b, _, idxp[here, :] = stream_tables(found[:, columns(1)], before)
        off_out[pl.ds(b, 1), :] = jnp.transpose(off_b)[:1, :]
        slot[pl.ds(b, 1), :] = jnp.transpose(slot_b)[:1, :]
        return carry

    lax.fori_loop(0, deck.shape[0] // RUN, block, 0)


def tables(runs, row_runs, info, deck, wet):
    slots = deck.shape[0]
    smem = pl.BlockSpec(memory_space=pltpu.SMEM)
    vmem = pl.BlockSpec(memory_space=pltpu.VMEM)
    i32 = lambda *shape: jax.ShapeDtypeStruct(shape, jnp.int32)

    def body(*refs):
        tables_kernel(runs, row_runs, *refs)

    return pl.pallas_call(
        body,
        in_specs=[smem, vmem, vmem],
        out_specs=[vmem] * 5,
        out_shape=[i32(slots, RUN)] * 2 + [i32(slots // RUN, RUN)] * 3,
        scratch_shapes=[pltpu.VMEM((slots, 2 * RUN), jnp.bfloat16)],
        cost_estimate=pl.CostEstimate(flops=4 * slots * slots * RUN, bytes_accessed=16 * slots * RUN, transcendentals=0),
        compiler_params=pltpu.CompilerParams(vmem_limit_bytes=VMEM_GRANT),
        name="tables",
    )(info, deck, wet)


def source_kernel(cap, runs, off, wind, limiter, ratio, growth, whitecap, idxp, code, decay, spectrum, held, *packed):
    groups = spectrum.shape[0] // SUB
    lane = lanes()
    block = groups * SUB
    grown = spread(growth[...].reshape(1, RUN))
    capped = spread(whitecap[...].reshape(1, RUN))
    spots = [place_all(off, q, runs, cap) for q in range(QUADRANTS)]
    for g in range(groups):
        q = g % QUADRANTS
        rows = slice(g * SUB, (g + 1) * SUB)
        values = []
        for t in range(runs):
            cols = columns(t)
            wind_t = jnp.broadcast_to(wind[:, cols], (SUB, RUN))
            limited = jnp.broadcast_to(limiter[:, cols], (SUB, RUN)) == 1
            values.append(
                force(spectrum[rows, cols], wind_t, ratio[:, cols], limited, grown[rows, :], capped[rows, :])
            )
        for t in range(runs):
            mark = rows_of(code, q * runs + t)
            kept = jnp.where(mark < DRY * RUN, decay[rows, :], 1.0)
            kept = jnp.where(mark < FLOWS_AND_STAYS * RUN, 0.0, kept)
            held[rows, columns(t)] = kept * values[t]
        if packed:
            sent = [lane_gather(values[t], rows_of(idxp, q * runs + t)) for t in range(runs)]

            def store(at, value, g=g):
                packed[0][g, at] = value

            write_stream(sent, spots[q], lane, store, cap)


def sources(cap, chunk, groups, pack, off, wind, limiter, ratio, growth, whitecap, idxp, code, decay, spectrum):
    points = spectrum.shape[1]
    runs = points // RUN
    block = RUN
    block_groups = block // SUB
    steps = groups // block_groups
    base = chunk * steps
    whole = lambda i: (0, 0)
    cells = groups * SUB * points

    def body(*refs):
        source_kernel(cap, runs, *refs)

    return pl.pallas_call(
        body,
        grid=(steps,),
        in_specs=[
            pl.BlockSpec(memory_space=pltpu.SMEM),
            pl.BlockSpec((1, points), whole),
            pl.BlockSpec((1, points), whole),
            pl.BlockSpec((SUB, points), whole),
            pl.BlockSpec((1, 1, RUN), lambda i: (base + i, 0, 0)),
            pl.BlockSpec((1, 1, RUN), lambda i: (base + i, 0, 0)),
            pl.BlockSpec((QUADRANTS * runs, RUN), whole),
            pl.BlockSpec((QUADRANTS * runs, RUN), whole),
            pl.BlockSpec((block, RUN), lambda i: (base + i, 0)),
            pl.BlockSpec((block, points), lambda i: (base + i, 0)),
        ],
        out_specs=[
            pl.BlockSpec((block, points), lambda i: (i, 0)),
            pl.BlockSpec((block_groups, cap, SUB, RUN), lambda i: (i, 0, 0, 0)),
        ][: 1 + pack],
        out_shape=[
            pltpu.HBM((groups * SUB, points), jnp.float32),
            pltpu.HBM((groups, cap, SUB, RUN), jnp.float32),
        ][: 1 + pack],
        cost_estimate=pl.CostEstimate(flops=10 * cells, bytes_accessed=12 * cells, transcendentals=2 * cells),
        compiler_params=pltpu.CompilerParams(vmem_limit_bytes=VMEM_GRANT),
        name="sources",
    )(off, wind, limiter, ratio, growth[:, None, :], whitecap[:, None, :], idxp, code, decay, spectrum)


def propagate_kernel(
    cap, runs, row_runs, slot, off_in, off_out, info, recv, idxu, idxp, wet, cx, cy, counts, sent, field, other, wide
):
    total = slot.shape[0]
    lane = lanes()
    blank = jnp.zeros((SUB, RUN), jnp.float32)
    for ref in (field, other):
        for q in range(row_runs):
            ref[q] = blank
            ref[row_runs + total + q] = blank

    span = 4 * SUB

    def spread_wet(i, carry):
        t0 = pl.multiple_of(i * span, SUB)
        block = wet[pl.ds(t0, span), :].astype(jnp.float32)
        for j in range(span):
            wide[t0 + j] = rows_of(block, j)
        return carry

    lax.fori_loop(0, total // span, spread_wet, 0)

    def unpack(i, carry):
        t0 = pl.multiple_of(i * runs, SUB)
        base = i * cap
        indices = idxu[pl.ds(t0, runs), :]
        done = []
        for j in range(runs):
            first, start = place(off_in[t0 + j], cap)
            second = jnp.minimum(first + 1, cap - 1)
            window = jnp.where(lane >= start, recv[base + first], recv[base + second])
            index = rows_of(indices, j)
            cells = lane_gather(window, jnp.bitwise_and(index, RUN - 1))
            done.append(jnp.where(index < RUN, cells, 0.0))
        for j in range(runs):
            field[row_runs + slot[t0 + j]] = done[j]
        return carry

    lax.fori_loop(0, total // runs, unpack, 0)

    up_row = info[0]
    last = info[2]
    block = 32 * row_runs

    def run_steps(eastward):
        edge = lane == (0 if eastward else RUN - 1)
        shift = 1 if eastward else RUN - 1

        def step(n, src, dst):
            on = n < counts[...]
            b = jnp.where(on, cx[...], 0.0)
            c = jnp.where(on, cy[...], 0.0)
            a = 1.0 - b - c

            def rows(i, inner):
                t0 = i * block
                here = src[pl.ds(row_runs + t0, block)]
                up_x = src[pl.ds(row_runs + t0 + up_row, block)]
                sea = wide[pl.ds(t0, block)]
                rolled = [pltpu.roll(here[k], shift, 1) for k in range(block)]
                out = []
                for k in range(block):
                    q = k % row_runs
                    near = rolled[k - q + (q - 1 if eastward else q + 1) % row_runs]
                    up_y = jnp.where(edge, near, rolled[k])
                    out.append(sea[k] * (a * here[k] + b * up_x[k] + c * up_y))
                dst[pl.ds(row_runs + t0, block)] = jnp.stack(out)
                return inner

            lax.fori_loop(0, total // block, rows, 0)

        def pair(m, carry):
            step(2 * m, field, other)
            step(2 * m + 1, other, field)
            return carry

        lax.fori_loop(0, (last + 1) // 2, pair, 0)

    @pl.when(info[1] > 0)
    def _():
        run_steps(True)

    @pl.when(info[1] <= 0)
    def _():
        run_steps(False)

    def pack(i, carry):
        t0 = pl.multiple_of(i * runs, SUB)
        indices = idxp[pl.ds(t0, runs), :]
        picked = [
            lane_gather(field[row_runs + slot[t0 + j]], rows_of(indices, j)) for j in range(runs)
        ]
        spots = [place(off_out[t0 + j], cap) for j in range(runs)]

        def store(at, value):
            sent[i * cap + at] = value

        write_stream(picked, spots, lane, store, cap)
        return carry

    lax.fori_loop(0, total // runs, pack, 0)


def propagate(cap, runs, row_runs, slot, off_in, off_out, info, recv, idxu, idxp, wet, cx, cy, counts):
    total = slot.shape[0]
    smem = pl.BlockSpec(memory_space=pltpu.SMEM)
    vmem = pl.BlockSpec(memory_space=pltpu.VMEM)
    cells = total * RUN * SUB

    def body(*refs):
        propagate_kernel(cap, runs, row_runs, *refs)

    padded = pltpu.VMEM((total + 2 * row_runs, SUB, RUN), jnp.float32)
    return pl.pallas_call(
        body,
        in_specs=[smem] * 4 + [vmem] * 7,
        out_specs=vmem,
        out_shape=jax.ShapeDtypeStruct(recv.shape, jnp.float32),
        scratch_shapes=[padded, padded, pltpu.VMEM((total, SUB, RUN), jnp.float32)],
        cost_estimate=pl.CostEstimate(flops=100 * cells, bytes_accessed=40 * cells, transcendentals=0),
        compiler_params=pltpu.CompilerParams(vmem_limit_bytes=VMEM_GRANT),
        name="propagate",
    )(slot, off_in, off_out, info, recv, idxu, idxp, wet, cx, cy, counts)


def finish_kernel(runs, comps, base, begin, end, off, code, recv, held, *rest):
    if begin:
        out, total, streams, values, stream_sems, value_sems, out_sems = rest
    elif end:
        before, _, out, height, streams, values, stream_sems, value_sems, out_sems, total = rest
    else:
        before, _, out, total, streams, values, stream_sems, value_sems, out_sems = rest
    lane = lanes()
    per, _, cap = recv.shape[:3]

    def arrive(q):
        return pltpu.make_async_copy(recv.at[:, q], streams.at[q, :, pl.ds(0, cap)], stream_sems.at[q])

    def bring(q):
        return pltpu.make_async_copy(held.at[:, q], values.at[q], value_sems.at[q])

    def leave(q):
        return pltpu.make_async_copy(values.at[q], out.at[pl.ds(base, per), q], out_sems.at[q])

    for q in range(QUADRANTS):
        arrive(q).start()
        bring(q).start()
    total[...] = jnp.zeros_like(total) if begin else before[...]
    for q in range(QUADRANTS):
        arrive(q).wait()
        bring(q).wait()
        here = streams.at[q]
        block = values.at[q]
        for t0 in range(0, runs, SUB):
            done = []
            for t in range(t0, t0 + SUB):
                offset = off[(q + 2) % QUADRANTS * runs + t, 0]
                first, start = split(offset)
                mark = rows_of(code, q * runs + t)
                comes = mark < STAYS * RUN
                index = jnp.bitwise_and(mark, RUN - 1)
                lower = lane >= start
                settled = []
                for m in range(per):
                    window = jnp.where(lower, here[m, first], here[m, first + 1])
                    cells = jnp.where(comes, lane_gather(window, index), 0.0)
                    settled.append(cells + block[m, :, columns(t)])
                done.append(settled)
            for k, settled in enumerate(done):
                cols = columns(t0 + k)
                for m in range(per):
                    block[m, :, cols] = settled[m]
                while len(settled) > 1:
                    settled = [sum(settled[n : n + 2]) for n in range(0, len(settled), 2)]
                total[:, cols] = total[:, cols] + settled[0]
        leave(q).start()
    if end:
        mean = jnp.sum(total[...], axis=0, keepdims=True) / comps
        mean = 4.0 * jnp.sqrt(mean + 1e-06)
        for t in range(runs):
            height[t : t + 1, :] = mean[:, columns(t)]
    for q in range(QUADRANTS):
        leave(q).wait()


def finish(cap, comps, chunk, begin, end, off, code, recv, held, before, out):
    block, points = held.shape
    runs = points // RUN
    per = block // SUB // QUADRANTS
    recv = recv.reshape(per, QUADRANTS, cap, SUB, RUN)
    held = held.reshape(per, QUADRANTS, SUB, points)
    smem = pl.BlockSpec(memory_space=pltpu.SMEM)
    whole = lambda *shape: pl.BlockSpec(shape, lambda i: (0, 0))
    far = pl.BlockSpec(memory_space=pltpu.HBM)
    specs = [smem, whole(QUADRANTS * runs, RUN), far, far]
    args = [off, code, recv, held]
    aliases = {}
    if not begin:
        specs += [whole(SUB, points), far]
        args += [before, out]
        aliases = {5: 0}
    cells = block * points
    last = (runs, RUN) if end else (SUB, points)

    def body(*refs):
        finish_kernel(runs, comps, chunk * per, begin, end, *refs)

    return pl.pallas_call(
        body,
        grid=(1,),
        in_specs=specs,
        out_specs=[far, whole(*last)],
        out_shape=[
            jax.ShapeDtypeStruct((comps // SUB // QUADRANTS, QUADRANTS, SUB, points), jnp.float32),
            jax.ShapeDtypeStruct(last, jnp.float32),
        ],
        scratch_shapes=[
            pltpu.VMEM((QUADRANTS, per, cap + 2, SUB, RUN), jnp.float32),
            pltpu.VMEM((QUADRANTS, per, SUB, points), jnp.float32),
            pltpu.SemaphoreType.DMA((QUADRANTS,)),
            pltpu.SemaphoreType.DMA((QUADRANTS,)),
            pltpu.SemaphoreType.DMA((QUADRANTS,)),
        ]
        + ([pltpu.VMEM((SUB, points), jnp.float32)] if end else []),
        input_output_aliases=aliases,
        cost_estimate=pl.CostEstimate(flops=4 * cells, bytes_accessed=12 * cells, transcendentals=0),
        compiler_params=pltpu.CompilerParams(vmem_limit_bytes=VMEM_GRANT),
        name="finish",
    )(*args)


def packed(spectrum, wind, growth, whitecap, courant, substeps, limiter, deck, wet):
    axes = ("pt", "comp")
    comp_count = lax.axis_size("comp")
    devices = lax.axis_size("pt") * comp_count
    rank = lax.axis_index("pt") * comp_count + lax.axis_index("comp")
    comps, points = spectrum.shape
    runs = points // RUN
    total = deck.shape[0] // RUN
    row_runs = wet.shape[1] // RUN
    chunks = comps // (devices * SUB)
    small = (runs * 3 + 3) // 4

    deck = deck.reshape(total, RUN)
    wind = wind[None, :]
    limiter = limiter[None, :]
    growth = growth.reshape(comps // RUN, RUN)
    whitecap = whitecap.reshape(comps // RUN, RUN)
    sent_small, sent_full, own_code, own_idxp, own_off, ratio, need = begin(
        small, runs, row_runs, devices, rank[None].astype(jnp.int32), deck, wet, wind, limiter,
        growth, whitecap, spectrum,
    )

    def branch(cap, first):
        def run(spectrum):
            all_cross, all_along = courants(jnp.arange(comps, dtype=jnp.int32), courant)
            decay = jnp.ones((comps,), jnp.float32)
            for n in range(MAXSUB):
                decay = jnp.where(n < substeps, decay * (1.0 - jnp.abs(all_cross) - jnp.abs(all_along)), decay)
            decay = jnp.broadcast_to(decay[:, None], (comps, RUN))
            kept = []
            received = []
            for chunk in range(chunks):
                held, *sent = sources(
                    cap, chunk, devices, chunk > 0, own_off, wind, limiter, ratio, growth, whitecap,
                    own_idxp, own_code, decay, spectrum,
                )
                kept.append(held)
                sent = sent[0] if sent else first.reshape(devices, cap, SUB, RUN)
                received.append(lax.all_to_all(sent, axes, split_axis=0, concat_axis=0, tiled=True))
            wet_runs = wet.reshape(total, RUN)
            returned = []
            for chunk in range(chunks):
                begin_at = (chunk * devices + rank) * SUB
                cross = lax.dynamic_slice_in_dim(all_cross, begin_at, SUB)
                along = lax.dynamic_slice_in_dim(all_along, begin_at, SUB)
                counts = lax.dynamic_slice_in_dim(substeps, begin_at, SUB)
                info = jnp.stack(
                    [
                        jnp.where(cross[0] > 0, -row_runs, row_runs),
                        jnp.where(along[0] > 0, 1, -1),
                        jnp.max(counts),
                    ]
                ).astype(jnp.int32)
                if chunk == 0:
                    idxu, idxp, off_in, off_out, slot = tables(runs, row_runs, info, deck, wet)
                    off_in, off_out, slot = (v.reshape(total) for v in (off_in, off_out, slot))
                wide = lambda v: jnp.broadcast_to(v[:, None], (SUB, RUN))
                sent = propagate(
                    cap, runs, row_runs, slot, off_in, off_out, info, received[chunk].reshape(devices * cap, SUB, RUN),
                    idxu, idxp, wet_runs, wide(jnp.abs(cross)), wide(jnp.abs(along)), wide(counts),
                )
                returned.append(
                    lax.all_to_all(
                        sent.reshape(devices, cap, SUB, RUN), axes, split_axis=0, concat_axis=0, tiled=True
                    )
                )
            out, sums = None, None
            for chunk in range(chunks):
                out, sums = finish(
                    cap, comps, chunk, chunk == 0, chunk == chunks - 1, own_off, own_code,
                    returned[chunk], kept[chunk], sums, out,
                )
            return out.reshape(comps, points), sums.reshape(points)

        return run

    return lax.cond(need[0] <= small * RUN, branch(small, sent_small), branch(runs, sent_full), spectrum)


def fits(spectrum, deck, wet, devices):
    comps, points = spectrum.shape
    runs = points // RUN
    return (
        comps % (devices * SUB) == 0
        and comps > devices * SUB
        and QUADRANTS * runs == RUN
        and devices % 16 == 0
        and runs % SUB == 0
        and RUN % runs == 0
        and wet.shape[0] % RUN == 0
        and deck.shape[0] % (RUN * RUN) == 0
    )


def on_device(spectrum, *rest):
    devices = lax.axis_size("pt") * lax.axis_size("comp")
    if fits(spectrum, *rest[-2:], devices):
        return packed(spectrum, *rest)
    return plain(spectrum, *rest)


def solution(mesh):
    in_specs = (
        P(None, ("pt", "comp")),
        P(("pt", "comp")),
        P(),
        P(),
        P(),
        P(),
        P(("pt", "comp")),
        P(),
        P(),
    )
    out_specs = (P(None, ("pt", "comp")), P(("pt", "comp")))
    return jax.shard_map(
        on_device, mesh=mesh, in_specs=in_specs, out_specs=out_specs, check_vma=False
    )
```
